32 devices in a mesh: dp: 8 (over y, x, core), expert: 4 (over z).
Axes of the slice: x: 2, y: 2, z: 4, core: 2. Of those that a mesh axis runs over, the one named last changes fastest.
Arguments:
- tokens: bfloat16 [1024, 2048], P('dp', 'expert'), may hold values from -6 to 6
- route_weight: bfloat16 [1024, 8], P('dp'), may hold values from 0.049804688 to 0.44921875
- expert_ids: int32 [1024, 8], P('dp'), may hold values from 0 to 7, all different within a row; in each aligned block of 128 rows (0 to 127, 128 to 255, ...) at most 128 rows name the same one
- gate_weight: bfloat16 [4, 1536, 2048], P('expert', 'dp'), may hold values from -0.125 to 0.125
- up_weight: bfloat16 [4, 1536, 2048], P('expert', 'dp'), may hold values from -0.125 to 0.125
- down_weight: bfloat16 [4, 1536, 2048], P('expert', 'dp'), may hold values from -0.21875 to 0.21875
- grad_output: bfloat16 [1024, 2048], P('dp', 'expert'), may hold values from -1.75 to 1.75
Outputs:
- mixed: bfloat16 [1024, 2048], P('dp', 'expert')
- grad_tokens: bfloat16 [1024, 2048], P('dp', 'expert')
- grad_route: float32 [1024, 8], P(('dp', 'expert'))
- grad_gate: bfloat16 [4, 1536, 2048], P('expert', 'dp')
- grad_up: bfloat16 [4, 1536, 2048], P('expert', 'dp')
- grad_down: bfloat16 [4, 1536, 2048], P('expert', 'dp')
The draws below stay inside these ranges and needn't reach their ends.
Inputs may be any that keep to these rules, and one draw needn't show every extreme that they name: `expert_ids`: each token names 8 different experts; among the 128 tokens of one device's aligned block no expert is named more than 128 times, a bound that some block reaches.
All inputs are finite; a program needn't handle non-finite values.
Results may differ from the reference program's by a relative error of at most 0.015.
Values may be sent and summed in bfloat16 or wider, within the bound.
A program may use at most 64 MiB of HBM per device.

```python
import math
import jax
import jax.numpy as jnp
import numpy as np
from jax import lax

D = 2048
FF = 768
TOPK = 8
PIECES = 4
TOK_DEV = 128
FFD = 192
EXP_DEV = 2
EXPERTS = 8
CAP = 128
TOKENS = 1024
N_DP = 8
N_EXPERT = 4


def block_levels(rng, shape, split, smallest, top_value):
    factor_of = 1.0
    for dim, shards_of in split:
        steps = jax.random.uniform(jax.random.fold_in(jax.random.fold_in(rng, 6), dim), (shards_of,), jnp.float32, smallest / len(split), top_value / len(split))
        factor_of = factor_of * jnp.repeat(jnp.exp(steps), shape[dim] // shards_of).reshape((-1,) + (1,) * (len(shape) - 1 - dim))
    return factor_of


def assign_block(key, own, number, rows, count, top, reach, skew):
    order = jax.random.permutation(key, count)
    crowded, usual = load_shares(count, rows * top, reach, skew, True), load_shares(count, rows * top, reach, skew, False)
    places = jnp.arange(count)

    def named(lengths, offset_by):
        used = int((lengths > 0).sum())
        fixed = max(1, used // 4)
        passed = fixed + (places - fixed + offset_by * (used - fixed)) % max(1, count - fixed)
        return jnp.zeros((count,), jnp.int32).at[order[jnp.where(places < fixed, places, passed)]].set(jnp.asarray(lengths, jnp.int32))

    lengths = jnp.where(number % 4 == 0, named(crowded, number // 4), named(usual, number - number // 4 - 1))
    mixed = jax.random.permutation(jax.random.fold_in(own, 3), count)
    giver, receiver = mixed[0:count // 2 * 2:2], mixed[1:count // 2 * 2:2]
    margin = jnp.minimum(lengths[giver] - 1, reach - lengths[receiver]) // 2
    margin = jnp.where((giver == order[0]) | (receiver == order[0]) | (lengths[receiver] == 0), 0, jnp.maximum(margin, 0))
    passed = jax.random.randint(jax.random.fold_in(own, 4), (count // 2,), 0, 1 << 20) % (margin + 1)
    lengths = lengths.at[giver].add(-passed).at[receiver].add(passed)
    items = jnp.searchsorted(jnp.cumsum(lengths), jnp.arange(rows * top), side="right").astype(jnp.int32)
    table = items.reshape(top, rows).T
    table = table[jax.random.permutation(jax.random.fold_in(own, 1), rows)]
    offset_by = jax.random.randint(jax.random.fold_in(own, 2), (rows, 1), 0, top)
    return jnp.take_along_axis(table, (jnp.arange(top)[None, :] + offset_by) % top, axis=1)


def load_shares(number_of, total, most, lean, full):
    weights = [(1 << 20) // math.isqrt(rank ** lean) + 1 for rank in range(1, number_of + 1)]
    largest = most if full else min(most, max(-(-total // number_of), total * weights[0] // sum(weights)))
    least = 1 if total - largest >= number_of - 1 else 0
    holding, rest = [largest] + [least] * (number_of - 1), total - largest - least * (number_of - 1)
    while rest > 0:
        free = [i for i in range(1, number_of) if holding[i] < largest] or [i for i in range(1, number_of) if holding[i] < most]
        pool, left = sum([weights[i] for i in free]), rest
        for i in free:
            extra = min(most - holding[i], max(1, left * weights[i] // pool), rest)
            holding[i] = holding[i] + extra
            rest = rest - extra
    return np.array(holding)


def noise(rng, shape, spread, limit, pieces=(), kind=jnp.bfloat16):
    entries = spread * jax.random.normal(rng, shape, jnp.float32)
    if pieces:
        entries = entries * block_levels(rng, shape, pieces, -0.22, 0.18)
    return jnp.clip(entries, -limit, limit).astype(kind)


def setup_inputs(seed: int = 0) -> dict:
    splits = jax.random.split(jax.random.key(seed), 8)
    tokens = noise(splits[0], (TOKENS, D), 1.0, 6.0, ((0, 8), (1, 4)))
    route_weight = jnp.clip(0.049804688 + 0.39941406 * jax.random.uniform(splits[1], (TOKENS, TOPK), jnp.float32) ** block_levels(splits[1], (TOKENS, TOPK), ((0, 8),), -0.2, 0.2), 0.049804688, 0.44921875).astype(jnp.bfloat16)
    expert_ids_keys = jax.random.split(jax.random.fold_in(splits[2], 1), TOKENS // TOK_DEV)
    expert_ids_turns = jax.random.permutation(jax.random.fold_in(splits[2], 3), TOKENS // TOK_DEV)
    expert_ids = jax.vmap(lambda own, number: assign_block(jax.random.fold_in(splits[2], 2), own, number, TOK_DEV, EXPERTS, TOPK, CAP, 2))(expert_ids_keys, expert_ids_turns).reshape((TOKENS, TOPK))
    gate_weight = noise(splits[3], (N_EXPERT, EXP_DEV * FF, D), D ** -0.5, 0.125, ((0, 4), (1, 8)))
    up_weight = noise(splits[4], (N_EXPERT, EXP_DEV * FF, D), D ** -0.5, 0.125, ((0, 4), (1, 8)))
    down_weight = noise(splits[5], (N_EXPERT, EXP_DEV * FF, D), FF ** -0.5, 0.21875, ((0, 4), (1, 8)))
    grad_output = noise(splits[6], (TOKENS, D), 0.3, 1.75, ((0, 8), (1, 4)))
    return dict(tokens=tokens, route_weight=route_weight, expert_ids=expert_ids, gate_weight=gate_weight, up_weight=up_weight, down_weight=down_weight, grad_output=grad_output)


def contract_last(left_side, right_side):
    return lax.dot_general(left_side, right_side, (((1,), (1,)), ((), ())), preferred_element_type=jnp.float32)


def contract_first(left_side, right_side):
    return lax.dot_general(left_side, right_side, (((0,), (0,)), ((), ())), preferred_element_type=jnp.float32)


def silu_parts(gate_act):
    sigmoid_val = jax.nn.sigmoid(gate_act)
    return gate_act * sigmoid_val, sigmoid_val * (1.0 + gate_act * (1.0 - sigmoid_val))


def slot_tables(expert_ids):
    block_rows = TOK_DEV * TOPK
    blocked = expert_ids.reshape(N_DP, block_rows)
    chosen = (blocked[:, :, None] == jnp.arange(EXPERTS, dtype=jnp.int32)[None, None, :]).astype(jnp.int32)
    slot_ranks = jnp.sum(chosen * (jnp.cumsum(chosen, axis=1) - 1), axis=2)
    starts = jnp.arange(N_DP, dtype=jnp.int32)[:, None] * CAP
    position = (starts + slot_ranks).reshape(-1).astype(jnp.int32)
    flat_ids = expert_ids.reshape(-1).astype(jnp.int32)
    row_index = jnp.arange(TOKENS * TOPK, dtype=jnp.int32)
    row_of = jnp.zeros((EXPERTS, N_DP * CAP), jnp.int32).at[flat_ids, position].set(row_index)
    slot_live = jnp.zeros((EXPERTS, N_DP * CAP), jnp.int32).at[flat_ids, position].set(jnp.ones_like(row_index))
    return row_of, slot_live


def reference(tokens, route_weight, expert_ids, gate_weight, up_weight, down_weight, grad_output):
    row_of, slot_live = slot_tables(expert_ids)
    flat_weight = route_weight.reshape(-1)
    gate_all = gate_weight.reshape(EXPERTS, PIECES, FFD, D)
    up_all = up_weight.reshape(EXPERTS, PIECES, FFD, D)
    down_all = down_weight.reshape(EXPERTS, PIECES, FFD, D)

    def per_expert(carry, item):
        mixed_sum, token_sum, route_sum = carry
        slot_row, live_row, gate_block, up_block, down_block = item
        slot_token = slot_row // TOPK
        keep_mask = live_row.astype(tokens.dtype)[:, None]
        slot_rows = tokens[slot_token] * keep_mask
        slot_grads = grad_output[slot_token] * keep_mask
        slot_scale = flat_weight[slot_row] * live_row.astype(route_weight.dtype)
        weight_wide = slot_scale.astype(jnp.float32)[:, None]
        scaled_grad = (weight_wide * slot_grads.astype(jnp.float32)).astype(jnp.bfloat16)
        out_total = jnp.zeros((N_DP * CAP, D), jnp.float32)
        grad_total = jnp.zeros((N_DP * CAP, D), jnp.float32)
        term_total = jnp.zeros((N_DP * CAP,), jnp.float32)
        gate_list = []
        up_list = []
        down_list = []
        for section in range(PIECES):
            gate_act = contract_last(slot_rows, gate_block[section])
            up_act = contract_last(slot_rows, up_block[section])
            active, silu_slope = silu_parts(gate_act)
            hidden = (active * up_act).astype(jnp.bfloat16)
            partial_out = jnp.dot(hidden, down_block[section], preferred_element_type=jnp.float32)
            piece_out = lax.optimization_barrier((weight_wide * partial_out).astype(jnp.bfloat16))
            out_total = out_total + piece_out.astype(jnp.float32)
            into_hidden = contract_last(slot_grads, down_block[section])
            route_term = jnp.sum(into_hidden * hidden.astype(jnp.float32), axis=1)
            route_term = lax.optimization_barrier(route_term.astype(jnp.bfloat16))
            term_total = term_total + route_term.astype(jnp.float32)
            hidden_grad = weight_wide * into_hidden
            gate_grad = (hidden_grad * up_act * silu_slope).astype(jnp.bfloat16)
            up_grad = (hidden_grad * active).astype(jnp.bfloat16)
            row_grad = jnp.dot(gate_grad, gate_block[section], preferred_element_type=jnp.float32) + jnp.dot(up_grad, up_block[section], preferred_element_type=jnp.float32)
            row_grad = lax.optimization_barrier(row_grad.astype(jnp.bfloat16))
            grad_total = grad_total + row_grad.astype(jnp.float32)
            gate_list.append(contract_first(gate_grad, slot_rows).astype(jnp.bfloat16))
            up_list.append(contract_first(up_grad, slot_rows).astype(jnp.bfloat16))
            down_list.append(contract_first(hidden, scaled_grad).astype(jnp.bfloat16))
        mixed_sum = mixed_sum.at[slot_token].add(out_total)
        token_sum = token_sum.at[slot_token].add(grad_total)
        route_sum = route_sum.at[slot_row].add(term_total)
        return (mixed_sum, token_sum, route_sum), (jnp.stack(gate_list), jnp.stack(up_list), jnp.stack(down_list))

    initial = (jnp.zeros((TOKENS, D), jnp.float32), jnp.zeros((TOKENS, D), jnp.float32), jnp.zeros((TOKENS * TOPK,), jnp.float32))
    totals, grads = lax.scan(per_expert, initial, (row_of, slot_live, gate_all, up_all, down_all))
    mixed_sum, token_sum, route_sum = totals
    gate_grads, up_grads, down_grads = grads
    grad_shape = (N_EXPERT, EXP_DEV * FF, D)
    return (mixed_sum.astype(jnp.bfloat16), token_sum.astype(jnp.bfloat16), route_sum.reshape(TOKENS, TOPK), gate_grads.reshape(grad_shape), up_grads.reshape(grad_shape), down_grads.reshape(grad_shape))
```

```python
import jax
import jax.numpy as jnp
from jax import lax
from jax.sharding import PartitionSpec as P

PIECES = 4


def contract_last(left_side, right_side):
    return lax.dot_general(
        left_side, right_side, (((1,), (1,)), ((), ())), preferred_element_type=jnp.float32
    )


def contract_first(left_side, right_side):
    return lax.dot_general(
        left_side, right_side, (((0,), (0,)), ((), ())), preferred_element_type=jnp.float32
    )


def silu_parts(gate_act):
    sigmoid_val = jax.nn.sigmoid(gate_act)
    return (gate_act * sigmoid_val, sigmoid_val * (1.0 + gate_act * (1.0 - sigmoid_val)))


def expert_forward(slot_rows, slot_scale, gate_piece, up_piece, down_piece):
    gate_act = contract_last(slot_rows, gate_piece)
    up_act = contract_last(slot_rows, up_piece)
    active, silu_slope = silu_parts(gate_act)
    hidden = (active * up_act).astype(jnp.bfloat16)
    partial_out = jnp.dot(hidden, down_piece, preferred_element_type=jnp.float32)
    scaled = (slot_scale.astype(jnp.float32)[:, None] * partial_out).astype(jnp.bfloat16)
    return (scaled, gate_act, up_act, hidden)


def slot_device(tokens, route_weight, expert_ids, gate_weight, up_weight, down_weight, grad_output):
    groups = lax.axis_size("expert")
    group_index = lax.axis_index("expert")
    data_size = lax.axis_size("dp")
    exp_local = data_size // PIECES
    tok_local, topk_count = expert_ids.shape
    capacity = min(tok_local, 2 * tok_local * topk_count // (exp_local * groups))
    full_tokens, full_grad = (
        lax.all_gather(tokens, "expert", axis=1, tiled=True),
        lax.all_gather(grad_output, "expert", axis=1, tiled=True),
    )
    feature_width = full_tokens.shape[1]
    gate_piece = gate_weight[0]
    up_piece = up_weight[0]
    down_piece = down_weight[0]
    flat_ids = expert_ids.reshape(-1)
    row_count = flat_ids.shape[0]
    owned_rows = flat_ids // exp_local == group_index
    local_ids = flat_ids % exp_local
    chosen = (
        (local_ids[:, None] == jnp.arange(exp_local, dtype=jnp.int32)[None, :])
        & owned_rows[:, None]
    ).astype(jnp.int32)
    slot_ranks = jnp.sum(chosen * (jnp.cumsum(chosen, axis=0) - 1), axis=1)
    slot_count = exp_local * capacity
    slot_pos = jnp.where(owned_rows, local_ids * capacity + slot_ranks, slot_count)
    row_index = jnp.arange(row_count, dtype=jnp.int32)
    row_of = jnp.zeros((slot_count,), jnp.int32).at[slot_pos].set(row_index, mode="drop")
    slot_live = (
        jnp.zeros((slot_count,), jnp.int32).at[slot_pos].set(jnp.ones_like(row_index), mode="drop")
    )
    token_of = row_of // topk_count
    keep_mask = slot_live.astype(tokens.dtype)[:, None]
    slot_weight = route_weight.reshape(-1)[row_of] * slot_live.astype(route_weight.dtype)

    def spread(values):
        trailing = values.shape[1:]
        grouped = values.reshape((exp_local, 1, capacity) + trailing)
        return jnp.broadcast_to(grouped, (exp_local, PIECES, capacity) + trailing).reshape(
            (data_size, capacity) + trailing
        )

    send_rows = spread(full_tokens[token_of] * keep_mask)
    send_weight = spread(slot_weight)
    send_grads = spread(full_grad[token_of] * keep_mask)
    recv_grads = None
    recv_scale = None
    recv_rows, recv_weight = (
        lax.all_to_all(send_rows, "dp", split_axis=0, concat_axis=0, tiled=True),
        lax.all_to_all(send_weight, "dp", split_axis=0, concat_axis=0, tiled=True),
    )
    scaled, gate_act, up_act, hidden = expert_forward(
        recv_rows.reshape(-1, feature_width),
        recv_weight.reshape(-1),
        gate_piece,
        up_piece,
        down_piece,
    )
    returned = lax.all_to_all(
        scaled.reshape(data_size, capacity, feature_width),
        "dp",
        split_axis=0,
        concat_axis=0,
        tiled=True,
    )
    slot_rows = recv_rows.reshape(-1, feature_width)
    wide_token = spread(token_of).reshape(-1)
    wide_live = spread(slot_live).reshape(-1)
    wide_row = spread(row_of).reshape(-1)
    token_place = (
        (wide_token[None, :] == jnp.arange(tok_local, dtype=jnp.int32)[:, None])
        & (wide_live[None, :] > 0)
    ).astype(jnp.bfloat16)
    mixed_sum = jnp.dot(
        token_place, returned.reshape(-1, feature_width), preferred_element_type=jnp.float32
    )
    recv_grads, recv_scale = (
        lax.all_to_all(send_grads, "dp", split_axis=0, concat_axis=0, tiled=True),
        lax.all_to_all(send_weight, "dp", split_axis=0, concat_axis=0, tiled=True),
    )
    active, silu_slope = silu_parts(gate_act)
    slot_grads = recv_grads.reshape(-1, feature_width)
    weight_wide = recv_scale.reshape(-1).astype(jnp.float32)[:, None]
    into_hidden = contract_last(slot_grads, down_piece)
    route_terms = jnp.sum(into_hidden * hidden.astype(jnp.float32), axis=1).astype(jnp.bfloat16)
    hidden_grad = weight_wide * into_hidden
    gate_grad = (hidden_grad * up_act * silu_slope).astype(jnp.bfloat16)
    up_grad = (hidden_grad * active).astype(jnp.bfloat16)
    row_grad = (
        jnp.dot(gate_grad, gate_piece, preferred_element_type=jnp.float32)
        + jnp.dot(up_grad, up_piece, preferred_element_type=jnp.float32)
    ).astype(jnp.bfloat16)
    scaled_grad = (weight_wide * slot_grads.astype(jnp.float32)).astype(jnp.bfloat16)
    grad_gate = contract_first(gate_grad, slot_rows).astype(jnp.bfloat16)[None]
    grad_up = contract_first(up_grad, slot_rows).astype(jnp.bfloat16)[None]
    grad_down = contract_first(hidden, scaled_grad).astype(jnp.bfloat16)[None]
    back_rows, back_terms = (
        lax.all_to_all(
            row_grad.reshape(data_size, capacity, feature_width),
            "dp",
            split_axis=0,
            concat_axis=0,
            tiled=True,
        ),
        lax.all_to_all(
            route_terms.reshape(data_size, capacity), "dp", split_axis=0, concat_axis=0, tiled=True
        ),
    )
    token_sum = jnp.dot(
        token_place, back_rows.reshape(-1, feature_width), preferred_element_type=jnp.float32
    )
    row_place = (
        (wide_row[None, :] == jnp.arange(row_count, dtype=jnp.int32)[:, None])
        & (wide_live[None, :] > 0)
    ).astype(jnp.bfloat16)
    route_sum = jnp.dot(
        row_place, back_terms.reshape(-1), preferred_element_type=jnp.float32
    ).reshape(tok_local, topk_count)
    mixed_part, token_part, route_part = (
        lax.psum_scatter(mixed_sum, "expert", scatter_dimension=1, tiled=True),
        lax.psum_scatter(token_sum, "expert", scatter_dimension=1, tiled=True),
        lax.psum_scatter(route_sum, "expert", scatter_dimension=0, tiled=True),
    )
    return (
        mixed_part.astype(jnp.bfloat16),
        token_part.astype(jnp.bfloat16),
        route_part,
        grad_gate,
        grad_up,
        grad_down,
    )


def dense_device(tokens, route_weight, expert_ids, gate_weight, up_weight, down_weight, grad_output):
    groups = lax.axis_size("expert")
    group_index = lax.axis_index("expert")
    data_size = lax.axis_size("dp")
    exp_local = data_size // PIECES
    experts = exp_local * groups
    own_expert = group_index * exp_local + lax.axis_index("dp") // PIECES
    gate_piece, up_piece, down_piece = gate_weight[0], up_weight[0], down_weight[0]
    names = jnp.arange(experts, dtype=jnp.int32)
    onehot = (expert_ids[:, :, None] == names).astype(jnp.float32)
    dense_weight = jnp.sum(onehot * route_weight.astype(jnp.float32)[:, :, None], axis=1)
    dense_weight = lax.all_gather(dense_weight, "dp", axis=0, tiled=True)
    weight_col = lax.dynamic_slice_in_dim(dense_weight, own_expert, 1, axis=1)
    gathered = lax.all_gather(tokens, "expert", axis=1, tiled=True)
    full_tokens = lax.all_gather(gathered, "dp", axis=0, tiled=True)
    gathered = lax.all_gather(grad_output, "expert", axis=1, tiled=True)
    full_grad = lax.all_gather(gathered, "dp", axis=0, tiled=True)
    gate_act = contract_last(full_tokens, gate_piece)
    up_act = contract_last(full_tokens, up_piece)
    active, slope = silu_parts(gate_act)
    hidden = active * up_act
    weighted = (weight_col * hidden).astype(jnp.bfloat16)
    mixed = jnp.dot(weighted, down_piece, preferred_element_type=jnp.float32).astype(jnp.bfloat16)
    into_hidden = contract_last(full_grad, down_piece)
    route_terms = jnp.sum(into_hidden * hidden, axis=1, keepdims=True)
    scaled = weight_col * into_hidden
    gate_grad = (scaled * up_act * slope).astype(jnp.bfloat16)
    up_grad = (scaled * active).astype(jnp.bfloat16)
    row_grad = (
        jnp.dot(gate_grad, gate_piece, preferred_element_type=jnp.float32)
        + jnp.dot(up_grad, up_piece, preferred_element_type=jnp.float32)
    ).astype(jnp.bfloat16)
    grad_gate = contract_first(gate_grad, full_tokens).astype(jnp.bfloat16)[None]
    grad_up = contract_first(up_grad, full_tokens).astype(jnp.bfloat16)[None]
    grad_down = contract_first(weighted, full_grad).astype(jnp.bfloat16)[None]

    def scatter(values, dim):
        values = lax.psum_scatter(values, "dp", scatter_dimension=0, tiled=True)
        return lax.psum_scatter(values, "expert", scatter_dimension=dim, tiled=True)

    route_wide = jnp.where(names[None, :] == own_expert, route_terms, 0.0)
    route_part = scatter(route_wide, 0)
    rows = route_part.shape[0]
    ids_part = lax.dynamic_slice_in_dim(expert_ids, group_index * rows, rows, axis=0)
    onehot_part = (ids_part[:, :, None] == names).astype(jnp.float32)
    grad_route = jnp.sum(onehot_part * route_part[:, None, :], axis=2)
    return (scatter(mixed, 1), scatter(row_grad, 1), grad_route, grad_gate, grad_up, grad_down)


def on_device(tokens, route_weight, expert_ids, *rest):
    experts = lax.axis_size("dp") // PIECES * lax.axis_size("expert")
    body = dense_device if experts == expert_ids.shape[1] else slot_device
    return body(tokens, route_weight, expert_ids, *rest)


def solution(mesh):
    return jax.shard_map(
        on_device,
        mesh=mesh,
        in_specs=(
            P("dp", "expert"),
            P("dp", None),
            P("dp", None),
            P("expert", "dp", None),
            P("expert", "dp", None),
            P("expert", "dp", None),
            P("dp", "expert"),
        ),
        out_specs=(
            P("dp", "expert"),
            P("dp", "expert"),
            P(("dp", "expert"), None),
            P("expert", "dp", None),
            P("expert", "dp", None),
            P("expert", "dp", None),
        ),
        check_vma=False,
    )
```

```python
import jax
import jax.numpy as jnp
from jax import lax
from jax.experimental import pallas as pl
from jax.experimental.pallas import tpu as pltpu
from jax.sharding import PartitionSpec as P

PIECES = 4


def contract_last(left_side, right_side):
    return lax.dot_general(
        left_side, right_side, (((1,), (1,)), ((), ())), preferred_element_type=jnp.float32
    )


def contract_first(left_side, right_side):
    return lax.dot_general(
        left_side, right_side, (((0,), (0,)), ((), ())), preferred_element_type=jnp.float32
    )


def silu_parts(gate_act):
    sigmoid_val = jax.nn.sigmoid(gate_act)
    return (gate_act * sigmoid_val, sigmoid_val * (1.0 + gate_act * (1.0 - sigmoid_val)))


def expert_forward(slot_rows, slot_scale, gate_piece, up_piece, down_piece):
    gate_act = contract_last(slot_rows, gate_piece)
    up_act = contract_last(slot_rows, up_piece)
    active, silu_slope = silu_parts(gate_act)
    hidden = (active * up_act).astype(jnp.bfloat16)
    partial_out = jnp.dot(hidden, down_piece, preferred_element_type=jnp.float32)
    scaled = (slot_scale.astype(jnp.float32)[:, None] * partial_out).astype(jnp.bfloat16)
    return (scaled, gate_act, up_act, hidden)


def slot_device(tokens, route_weight, expert_ids, gate_weight, up_weight, down_weight, grad_output):
    groups = lax.axis_size("expert")
    group_index = lax.axis_index("expert")
    data_size = lax.axis_size("dp")
    exp_local = data_size // PIECES
    tok_local, topk_count = expert_ids.shape
    capacity = min(tok_local, 2 * tok_local * topk_count // (exp_local * groups))
    full_tokens, full_grad = (
        lax.all_gather(tokens, "expert", axis=1, tiled=True),
        lax.all_gather(grad_output, "expert", axis=1, tiled=True),
    )
    feature_width = full_tokens.shape[1]
    gate_piece = gate_weight[0]
    up_piece = up_weight[0]
    down_piece = down_weight[0]
    flat_ids = expert_ids.reshape(-1)
    row_count = flat_ids.shape[0]
    owned_rows = flat_ids // exp_local == group_index
    local_ids = flat_ids % exp_local
    chosen = (
        (local_ids[:, None] == jnp.arange(exp_local, dtype=jnp.int32)[None, :])
        & owned_rows[:, None]
    ).astype(jnp.int32)
    slot_ranks = jnp.sum(chosen * (jnp.cumsum(chosen, axis=0) - 1), axis=1)
    slot_count = exp_local * capacity
    slot_pos = jnp.where(owned_rows, local_ids * capacity + slot_ranks, slot_count)
    row_index = jnp.arange(row_count, dtype=jnp.int32)
    row_of = jnp.zeros((slot_count,), jnp.int32).at[slot_pos].set(row_index, mode="drop")
    slot_live = (
        jnp.zeros((slot_count,), jnp.int32).at[slot_pos].set(jnp.ones_like(row_index), mode="drop")
    )
    token_of = row_of // topk_count
    keep_mask = slot_live.astype(tokens.dtype)[:, None]
    slot_weight = route_weight.reshape(-1)[row_of] * slot_live.astype(route_weight.dtype)

    def spread(values):
        trailing = values.shape[1:]
        grouped = values.reshape((exp_local, 1, capacity) + trailing)
        return jnp.broadcast_to(grouped, (exp_local, PIECES, capacity) + trailing).reshape(
            (data_size, capacity) + trailing
        )

    send_rows = spread(full_tokens[token_of] * keep_mask)
    send_weight = spread(slot_weight)
    send_grads = spread(full_grad[token_of] * keep_mask)
    recv_grads = None
    recv_scale = None
    recv_rows, recv_weight = (
        lax.all_to_all(send_rows, "dp", split_axis=0, concat_axis=0, tiled=True),
        lax.all_to_all(send_weight, "dp", split_axis=0, concat_axis=0, tiled=True),
    )
    scaled, gate_act, up_act, hidden = expert_forward(
        recv_rows.reshape(-1, feature_width),
        recv_weight.reshape(-1),
        gate_piece,
        up_piece,
        down_piece,
    )
    returned = lax.all_to_all(
        scaled.reshape(data_size, capacity, feature_width),
        "dp",
        split_axis=0,
        concat_axis=0,
        tiled=True,
    )
    slot_rows = recv_rows.reshape(-1, feature_width)
    wide_token = spread(token_of).reshape(-1)
    wide_live = spread(slot_live).reshape(-1)
    wide_row = spread(row_of).reshape(-1)
    token_place = (
        (wide_token[None, :] == jnp.arange(tok_local, dtype=jnp.int32)[:, None])
        & (wide_live[None, :] > 0)
    ).astype(jnp.bfloat16)
    mixed_sum = jnp.dot(
        token_place, returned.reshape(-1, feature_width), preferred_element_type=jnp.float32
    )
    recv_grads, recv_scale = (
        lax.all_to_all(send_grads, "dp", split_axis=0, concat_axis=0, tiled=True),
        lax.all_to_all(send_weight, "dp", split_axis=0, concat_axis=0, tiled=True),
    )
    active, silu_slope = silu_parts(gate_act)
    slot_grads = recv_grads.reshape(-1, feature_width)
    weight_wide = recv_scale.reshape(-1).astype(jnp.float32)[:, None]
    into_hidden = contract_last(slot_grads, down_piece)
    route_terms = jnp.sum(into_hidden * hidden.astype(jnp.float32), axis=1).astype(jnp.bfloat16)
    hidden_grad = weight_wide * into_hidden
    gate_grad = (hidden_grad * up_act * silu_slope).astype(jnp.bfloat16)
    up_grad = (hidden_grad * active).astype(jnp.bfloat16)
    row_grad = (
        jnp.dot(gate_grad, gate_piece, preferred_element_type=jnp.float32)
        + jnp.dot(up_grad, up_piece, preferred_element_type=jnp.float32)
    ).astype(jnp.bfloat16)
    scaled_grad = (weight_wide * slot_grads.astype(jnp.float32)).astype(jnp.bfloat16)
    grad_gate = contract_first(gate_grad, slot_rows).astype(jnp.bfloat16)[None]
    grad_up = contract_first(up_grad, slot_rows).astype(jnp.bfloat16)[None]
    grad_down = contract_first(hidden, scaled_grad).astype(jnp.bfloat16)[None]
    back_rows, back_terms = (
        lax.all_to_all(
            row_grad.reshape(data_size, capacity, feature_width),
            "dp",
            split_axis=0,
            concat_axis=0,
            tiled=True,
        ),
        lax.all_to_all(
            route_terms.reshape(data_size, capacity), "dp", split_axis=0, concat_axis=0, tiled=True
        ),
    )
    token_sum = jnp.dot(
        token_place, back_rows.reshape(-1, feature_width), preferred_element_type=jnp.float32
    )
    row_place = (
        (wide_row[None, :] == jnp.arange(row_count, dtype=jnp.int32)[:, None])
        & (wide_live[None, :] > 0)
    ).astype(jnp.bfloat16)
    route_sum = jnp.dot(
        row_place, back_terms.reshape(-1), preferred_element_type=jnp.float32
    ).reshape(tok_local, topk_count)
    mixed_part, token_part, route_part = (
        lax.psum_scatter(mixed_sum, "expert", scatter_dimension=1, tiled=True),
        lax.psum_scatter(token_sum, "expert", scatter_dimension=1, tiled=True),
        lax.psum_scatter(route_sum, "expert", scatter_dimension=0, tiled=True),
    )
    return (
        mixed_part.astype(jnp.bfloat16),
        token_part.astype(jnp.bfloat16),
        route_part,
        grad_gate,
        grad_up,
        grad_down,
    )


MESH = pl.DeviceIdType.MESH
GATHER_ORDER = (0, 1, 3, 2)
SCATTER_ORDER = (2, 1, 3, 0)


def remote(src, dst, sems, index, device):
    return pltpu.make_async_remote_copy(
        src_ref=src,
        dst_ref=dst,
        send_sem=sems.at[(0,) + index],
        recv_sem=sems.at[(1,) + index],
        device_id=device,
        device_id_type=MESH,
    )


def dense_kernel(
    tok_ref, rw_ref, ids_ref, wg_ref, wu_ref, wd_ref, gy_ref,
    mixed_ref, token_ref, route_ref, gg_ref, gu_ref, gd_ref,
    acts, parts, weights, wide, gate, up, into, hw, gg, ug, turned,
    half_in, full_in, z_out, z_in, z_own, route, route_in, route_sum, route_z, wg_out, wg_in,
    s_z, s_plane, s_fwd, s_wide, s_wt, s_local, s_r1, s_r2, s_r3, s_rt, s_rz, s_wg,
):
    f32, bf16 = jnp.float32, jnp.bfloat16
    rows, feat = tok_ref.shape
    unit = wg_ref.shape[1]
    topk = ids_ref.shape[1]
    half = rows // 2
    quarters = acts.shape[1]
    d, z = lax.axis_index("dp"), lax.axis_index("expert")
    core, x, y = lax.rem(d, 2), lax.rem(d // 2, 2), d // 4
    x_dev = (y * 4 + (1 - x) * 2 + core, z)
    y_dev = ((1 - y) * 4 + x * 2 + core, z)
    diag_dev = ((1 - y) * 4 + (1 - x) * 2 + core, z)
    twin = (y * 4 + x * 2 + (1 - core), z)
    expert = z * (lax.axis_size("dp") // PIECES) + d // PIECES

    def quarter(r):
        return lax.rem(z + r, quarters)

    def z_dev(r):
        return (d, quarter(r))

    barrier = pltpu.get_barrier_semaphore()
    others = [x_dev, y_dev, diag_dev, twin] + [z_dev(r) for r in range(1, quarters)]
    for dev in others:
        pl.semaphore_signal(barrier, inc=1, device_id=dev, device_id_type=MESH)
    pl.semaphore_wait(barrier, len(others))

    own, at_x, at_y, at_d = (pl.ds(i * rows, rows) for i in range(4))
    d_top, d_low = pl.ds(3 * rows, half), pl.ds(3 * rows + half, half)
    x_top, x_low = pl.ds(rows, half), pl.ds(rows + half, half)
    y_top, y_low = pl.ds(2 * rows, half), pl.ds(2 * rows + half, half)
    started = []

    def go(copy):
        copy.start()
        started.append(copy)

    def z_send(a, s):
        block = acts.at[a, z, own]
        return remote(block, block, s_z, (a, quarters - 1 - s), z_dev(s))

    def z_arrive(a, r):
        block = acts.at[a, quarter(r), own]
        remote(block, block, s_z, (a, r - 1), z_dev(r)).wait_recv()

    def plane(a, r):
        q = quarter(r)
        src = acts.at[a, q, own]
        return (
            remote(src, acts.at[a, q, at_x], s_plane, (a, 0, r), x_dev),
            remote(src, acts.at[a, q, at_y], s_plane, (a, 1, r), y_dev),
        )

    def forward(a, r):
        q = quarter(r)
        return (
            remote(acts.at[a, q, x_top], acts.at[a, q, d_top], s_fwd, (a, 0, r), y_dev),
            remote(acts.at[a, q, y_low], acts.at[a, q, d_low], s_fwd, (a, 1, r), x_dev),
        )

    def send_plane(a, r):
        for copy in plane(a, r):
            go(copy)

    def pass_on(a, r):
        for arrived, onward in zip(plane(a, r), forward(a, r)):
            arrived.wait_recv()
            go(onward)

    def complete(a, r):
        for copy in forward(a, r):
            copy.wait_recv()

    acts[0, z, own, :] = tok_ref[...]
    acts[1, z, own, :] = gy_ref[...]
    for s in (1, 3, 2):
        go(z_send(0, s))
    send_plane(0, 0)
    local, lent = [], []
    for m, ref in enumerate((wg_ref, wu_ref, wd_ref)):
        copy = pltpu.make_async_copy(ref.at[0], weights.at[m, pl.ds(0, unit)], s_local.at[m])
        copy.start()
        local.append(copy)
        lent.append(remote(ref.at[0], weights.at[m, pl.ds(unit, unit)], s_wt, (m,), twin))
        go(lent[m])

    lane = lax.broadcasted_iota(jnp.int32, (rows, 128), 1)
    ids, rw = ids_ref[...], rw_ref[...].astype(f32)
    spread = jnp.zeros((rows, 128), f32)
    for k in range(topk):
        spread = spread + jnp.where(lane == ids[:, k : k + 1], rw[:, k : k + 1], 0.0)
    wide[own, :] = spread
    wide_copies = [
        remote(wide.at[own], wide.at[place], s_wide, (i,), dev)
        for i, (place, dev) in enumerate(((at_x, x_dev), (at_y, y_dev), (at_d, diag_dev)))
    ]
    for copy in wide_copies:
        go(copy)
    for s in (1, 3, 2):
        go(z_send(1, s))
    for r in GATHER_ORDER[1:]:
        z_arrive(0, r)
        send_plane(0, r)
    for m in range(3):
        local[m].wait()
        lent[m].wait_recv()

    def columns(q):
        return pl.ds(pl.multiple_of(q * feat, feat), feat)

    def add_forward(i, r):
        q = quarter(r)
        for total, m in ((gate, 0), (up, 1)):
            term = contract_last(acts[0, q], weights[m, :, columns(q)])
            total[...] = term if i == 0 else total[...] + term

    for i, r in enumerate(GATHER_ORDER):
        pass_on(0, r)
        if i > 0:
            z_arrive(1, r)
        send_plane(1, r)
        if i > 0:
            complete(0, GATHER_ORDER[i - 1])
            add_forward(i - 1, GATHER_ORDER[i - 1])
    complete(0, GATHER_ORDER[-1])
    add_forward(len(GATHER_ORDER) - 1, GATHER_ORDER[-1])
    for copy in wide_copies:
        copy.wait_recv()

    def block_rows(b):
        return pl.ds(pl.multiple_of(b * rows, rows), rows)

    def scale_of(b):
        return jnp.sum(jnp.where(lane == expert, wide[block_rows(b), :], 0.0), axis=1, keepdims=True)

    @pl.loop(0, 4)
    def _(b):
        at = block_rows(b)
        active, _slope = silu_parts(gate[at, :])
        weighted = scale_of(b) * (active * up[at, :])
        hw[at, :] = weighted.astype(bf16)
        turned[2, :, at] = weighted.T.astype(bf16)

    def first(a, r):
        q = quarter(r)
        return (
            remote(parts.at[a, q, d_top], half_in.at[a, 0, r], s_r1, (a, 0, r), x_dev),
            remote(parts.at[a, q, d_low], half_in.at[a, 1, r], s_r1, (a, 1, r), y_dev),
        )

    def second(a, r):
        q = quarter(r)
        return (
            remote(parts.at[a, q, at_x], full_in.at[a, 0, r], s_r2, (a, 0, r), x_dev),
            remote(parts.at[a, q, at_y], full_in.at[a, 1, r], s_r2, (a, 1, r), y_dev),
        )

    def send_first(a, r):
        for copy in first(a, r):
            go(copy)

    def add_first(a, r):
        q = quarter(r)
        for i, (copy, place) in enumerate(zip(first(a, r), (y_top, x_low))):
            copy.wait_recv()
            here = parts[a, q, place, :].astype(f32) + half_in[a, i, r].astype(f32)
            parts[a, q, place, :] = here.astype(bf16)
        for copy in second(a, r):
            go(copy)

    def third(a, r):
        return remote(z_out.at[a, r - 1], z_in.at[a, quarters - 1 - r], s_r3, (a, quarters - 1 - r), z_dev(r))

    def add_second(a, r):
        for copy in second(a, r):
            copy.wait_recv()
        total = parts[a, quarter(r), own, :].astype(f32)
        total = total + full_in[a, 0, r].astype(f32) + full_in[a, 1, r].astype(f32)
        if r == 0:
            z_own[a] = total
        else:
            z_out[a, r - 1] = total.astype(bf16)
            go(third(a, r))

    def finish(a, out_ref):
        total = z_own[a]
        for r in range(1, quarters):
            slot = z_in.at[a, r - 1]
            remote(slot, slot, s_r3, (a, r - 1), z_dev(r)).wait_recv()
            total = total + z_in[a, r - 1].astype(f32)
        out_ref[...] = total.astype(bf16)

    for near, r in zip(GATHER_ORDER, SCATTER_ORDER):
        q = quarter(r)
        pass_on(1, near)
        parts[0, q] = jnp.dot(
            hw[...], weights[2, :, columns(q)], preferred_element_type=f32
        ).astype(bf16)
        send_first(0, r)

    for i, (near, r) in enumerate(zip(GATHER_ORDER, SCATTER_ORDER)):
        q = quarter(near)
        complete(1, near)
        term = contract_last(acts[1, q], weights[2, :, columns(q)])
        into[...] = term if i == 0 else into[...] + term
        add_first(0, r)

    @pl.loop(0, 4)
    def _(b):
        at = block_rows(b)
        gate_act, up_act, back = gate[at, :], up[at, :], into[at, :]
        active, slope = silu_parts(gate_act)
        term = jnp.sum(back * (active * up_act), axis=1, keepdims=True)
        route[at, :] = jnp.where(lane == expert, term, 0.0)
        scaled = scale_of(b) * back
        gate_grad, up_grad = scaled * up_act * slope, scaled * active
        gg[at, :] = gate_grad.astype(bf16)
        ug[at, :] = up_grad.astype(bf16)
        turned[0, :, at] = gate_grad.T.astype(bf16)
        turned[1, :, at] = up_grad.T.astype(bf16)

    for r in SCATTER_ORDER:
        q = quarter(r)
        total = jnp.dot(gg[...], weights[0, :, columns(q)], preferred_element_type=f32)
        total = total + jnp.dot(ug[...], weights[1, :, columns(q)], preferred_element_type=f32)
        parts[1, q] = total.astype(bf16)
        send_first(1, r)
        add_second(0, r)

    route_copies = [
        remote(route.at[place], route_in.at[i], s_rt, (i,), dev)
        for i, (place, dev) in enumerate(((at_x, x_dev), (at_y, y_dev), (at_d, diag_dev)))
    ]
    for copy in route_copies:
        go(copy)

    lent_grads = []
    for m in range(3):
        @pl.loop(0, quarters)
        def _(q, m=m):
            wg_out[m, :, columns(q)] = jnp.dot(
                turned[m, pl.ds(unit, unit), :], acts[m // 2, q], preferred_element_type=f32
            ).astype(bf16)

        lent_grads.append(remote(wg_out.at[m], wg_in.at[m], s_wg, (m,), twin))
        go(lent_grads[m])

    for r in SCATTER_ORDER:
        add_first(1, r)

    for copy in route_copies:
        copy.wait_recv()
    route_sum[...] = route[own, :] + route_in[0] + route_in[1] + route_in[2]
    slab = rows // quarters

    def slab_of(q):
        return pl.ds(pl.multiple_of(q * slab, slab), slab)

    for s in range(1, quarters):
        go(remote(route_sum.at[slab_of(quarter(s))], route_z.at[quarters - 1 - s], s_rz, (quarters - 1 - s,), z_dev(s)))

    for m, out_ref in enumerate((gg_ref, gu_ref, gd_ref)):
        lent_grads[m].wait_recv()

        @pl.loop(0, quarters)
        def _(q, m=m, out_ref=out_ref):
            total = jnp.dot(turned[m, pl.ds(0, unit), :], acts[m // 2, q], preferred_element_type=f32)
            out_ref[0, :, columns(q)] = (total + wg_in[m, :, columns(q)].astype(f32)).astype(bf16)

    finish(0, mixed_ref)
    for r in SCATTER_ORDER:
        add_second(1, r)

    total = route_sum[slab_of(z), :]
    for r in range(1, quarters):
        slot = route_z.at[r - 1]
        remote(slot, slot, s_rz, (r - 1,), z_dev(r)).wait_recv()
        total = total + route_z[r - 1]
    names = ids_ref[slab_of(z), :]
    lane_slab = lax.broadcasted_iota(jnp.int32, (slab, 128), 1)
    lane_k = lax.broadcasted_iota(jnp.int32, (slab, topk), 1)
    picked = jnp.zeros((slab, topk), f32)
    for k in range(topk):
        value = jnp.sum(jnp.where(lane_slab == names[:, k : k + 1], total, 0.0), axis=1, keepdims=True)
        picked = jnp.where(lane_k == k, value, picked)
    route_ref[...] = picked
    finish(1, token_ref)
    for copy in started:
        copy.wait_send()


def dense_device(tokens, route_weight, expert_ids, gate_weight, up_weight, down_weight, grad_output):
    quarters = lax.axis_size("expert")
    rows, feat = tokens.shape
    unit, width = gate_weight.shape[1:]
    topk = expert_ids.shape[1]
    f32, bf16 = jnp.float32, jnp.bfloat16
    vmem = pl.BlockSpec(memory_space=pltpu.VMEM)
    hbm = pl.BlockSpec(memory_space=pl.ANY)
    every, both, half = 4 * rows, 2 * unit, rows // 2
    dma = pltpu.SemaphoreType.DMA
    grads = jax.ShapeDtypeStruct((1, unit, width), bf16)
    return pl.pallas_call(
        dense_kernel,
        out_shape=(
            jax.ShapeDtypeStruct((rows, feat), bf16),
            jax.ShapeDtypeStruct((rows, feat), bf16),
            jax.ShapeDtypeStruct((rows // quarters, topk), f32),
            grads,
            grads,
            grads,
        ),
        in_specs=[vmem, vmem, vmem, hbm, hbm, hbm, vmem],
        out_specs=(vmem,) * 6,
        scratch_shapes=[
            pltpu.VMEM((2, quarters, every, feat), bf16),
            pltpu.VMEM((2, quarters, every, feat), bf16),
            pltpu.VMEM((3, both, width), bf16),
            pltpu.VMEM((every, 128), f32),
            pltpu.VMEM((every, both), f32),
            pltpu.VMEM((every, both), f32),
            pltpu.VMEM((every, both), f32),
            pltpu.VMEM((every, both), bf16),
            pltpu.VMEM((every, both), bf16),
            pltpu.VMEM((every, both), bf16),
            pltpu.VMEM((3, both, every), bf16),
            pltpu.VMEM((2, 2, quarters, half, feat), bf16),
            pltpu.VMEM((2, 2, quarters, rows, feat), bf16),
            pltpu.VMEM((2, quarters - 1, rows, feat), bf16),
            pltpu.VMEM((2, quarters - 1, rows, feat), bf16),
            pltpu.VMEM((2, rows, feat), f32),
            pltpu.VMEM((every, 128), f32),
            pltpu.VMEM((3, rows, 128), f32),
            pltpu.VMEM((rows, 128), f32),
            pltpu.VMEM((quarters - 1, rows // quarters, 128), f32),
            pltpu.VMEM((3, unit, width), bf16),
            pltpu.VMEM((3, unit, width), bf16),
            dma((2, 2, quarters - 1)),
            dma((2, 2, 2, quarters)),
            dma((2, 2, 2, quarters)),
            dma((2, 3)),
            dma((2, 3)),
            dma((3,)),
            dma((2, 2, 2, quarters)),
            dma((2, 2, 2, quarters)),
            dma((2, 2, quarters - 1)),
            dma((2, 3)),
            dma((2, quarters - 1)),
            dma((2, 3)),
        ],
        compiler_params=pltpu.CompilerParams(
            collective_id=0, has_side_effects=True, vmem_limit_bytes=52 * 2**20
        ),
        cost_estimate=pl.CostEstimate(
            flops=18 * every * both * width, bytes_accessed=12 * unit * width, transcendentals=2 * every * both
        ),
    )(tokens, route_weight, expert_ids, gate_weight, up_weight, down_weight, grad_output)


def on_device(tokens, route_weight, expert_ids, *rest):
    shape = (lax.axis_size("dp"), lax.axis_size("expert"))
    experts = shape[0] // PIECES * shape[1]
    dense = shape == (8, 4) and experts == expert_ids.shape[1]
    body = dense_device if dense else slot_device
    return body(tokens, route_weight, expert_ids, *rest)


def solution(mesh):
    return jax.shard_map(
        on_device,
        mesh=mesh,
        in_specs=(
            P("dp", "expert"),
            P("dp", None),
            P("dp", None),
            P("expert", "dp", None),
            P("expert", "dp", None),
            P("expert", "dp", None),
            P("dp", "expert"),
        ),
        out_specs=(
            P("dp", "expert"),
            P("dp", "expert"),
            P(("dp", "expert"), None),
            P("expert", "dp", None),
            P("expert", "dp", None),
            P("expert", "dp", None),
        ),
        check_vma=False,
    )
```

```python
import jax
import jax.numpy as jnp
from jax import lax
from jax.experimental import pallas as pl
from jax.experimental.pallas import tpu as pltpu
from jax.sharding import PartitionSpec as P

PIECES = 4


def contract_last(left_side, right_side):
    return lax.dot_general(
        left_side, right_side, (((1,), (1,)), ((), ())), preferred_element_type=jnp.float32
    )


def contract_first(left_side, right_side):
    return lax.dot_general(
        left_side, right_side, (((0,), (0,)), ((), ())), preferred_element_type=jnp.float32
    )


def silu_parts(gate_act):
    sigmoid_val = jax.nn.sigmoid(gate_act)
    return (gate_act * sigmoid_val, sigmoid_val * (1.0 + gate_act * (1.0 - sigmoid_val)))


def expert_forward(slot_rows, slot_scale, gate_piece, up_piece, down_piece):
    gate_act = contract_last(slot_rows, gate_piece)
    up_act = contract_last(slot_rows, up_piece)
    active, silu_slope = silu_parts(gate_act)
    hidden = (active * up_act).astype(jnp.bfloat16)
    partial_out = jnp.dot(hidden, down_piece, preferred_element_type=jnp.float32)
    scaled = (slot_scale.astype(jnp.float32)[:, None] * partial_out).astype(jnp.bfloat16)
    return (scaled, gate_act, up_act, hidden)


def slot_device(tokens, route_weight, expert_ids, gate_weight, up_weight, down_weight, grad_output):
    groups = lax.axis_size("expert")
    group_index = lax.axis_index("expert")
    data_size = lax.axis_size("dp")
    exp_local = data_size // PIECES
    tok_local, topk_count = expert_ids.shape
    capacity = min(tok_local, 2 * tok_local * topk_count // (exp_local * groups))
    full_tokens, full_grad = (
        lax.all_gather(tokens, "expert", axis=1, tiled=True),
        lax.all_gather(grad_output, "expert", axis=1, tiled=True),
    )
    feature_width = full_tokens.shape[1]
    gate_piece = gate_weight[0]
    up_piece = up_weight[0]
    down_piece = down_weight[0]
    flat_ids = expert_ids.reshape(-1)
    row_count = flat_ids.shape[0]
    owned_rows = flat_ids // exp_local == group_index
    local_ids = flat_ids % exp_local
    chosen = (
        (local_ids[:, None] == jnp.arange(exp_local, dtype=jnp.int32)[None, :])
        & owned_rows[:, None]
    ).astype(jnp.int32)
    slot_ranks = jnp.sum(chosen * (jnp.cumsum(chosen, axis=0) - 1), axis=1)
    slot_count = exp_local * capacity
    slot_pos = jnp.where(owned_rows, local_ids * capacity + slot_ranks, slot_count)
    row_index = jnp.arange(row_count, dtype=jnp.int32)
    row_of = jnp.zeros((slot_count,), jnp.int32).at[slot_pos].set(row_index, mode="drop")
    slot_live = (
        jnp.zeros((slot_count,), jnp.int32).at[slot_pos].set(jnp.ones_like(row_index), mode="drop")
    )
    token_of = row_of // topk_count
    keep_mask = slot_live.astype(tokens.dtype)[:, None]
    slot_weight = route_weight.reshape(-1)[row_of] * slot_live.astype(route_weight.dtype)

    def spread(values):
        trailing = values.shape[1:]
        grouped = values.reshape((exp_local, 1, capacity) + trailing)
        return jnp.broadcast_to(grouped, (exp_local, PIECES, capacity) + trailing).reshape(
            (data_size, capacity) + trailing
        )

    send_rows = spread(full_tokens[token_of] * keep_mask)
    send_weight = spread(slot_weight)
    send_grads = spread(full_grad[token_of] * keep_mask)
    recv_grads = None
    recv_scale = None
    recv_rows, recv_weight = (
        lax.all_to_all(send_rows, "dp", split_axis=0, concat_axis=0, tiled=True),
        lax.all_to_all(send_weight, "dp", split_axis=0, concat_axis=0, tiled=True),
    )
    scaled, gate_act, up_act, hidden = expert_forward(
        recv_rows.reshape(-1, feature_width),
        recv_weight.reshape(-1),
        gate_piece,
        up_piece,
        down_piece,
    )
    returned = lax.all_to_all(
        scaled.reshape(data_size, capacity, feature_width),
        "dp",
        split_axis=0,
        concat_axis=0,
        tiled=True,
    )
    slot_rows = recv_rows.reshape(-1, feature_width)
    wide_token = spread(token_of).reshape(-1)
    wide_live = spread(slot_live).reshape(-1)
    wide_row = spread(row_of).reshape(-1)
    token_place = (
        (wide_token[None, :] == jnp.arange(tok_local, dtype=jnp.int32)[:, None])
        & (wide_live[None, :] > 0)
    ).astype(jnp.bfloat16)
    mixed_sum = jnp.dot(
        token_place, returned.reshape(-1, feature_width), preferred_element_type=jnp.float32
    )
    recv_grads, recv_scale = (
        lax.all_to_all(send_grads, "dp", split_axis=0, concat_axis=0, tiled=True),
        lax.all_to_all(send_weight, "dp", split_axis=0, concat_axis=0, tiled=True),
    )
    active, silu_slope = silu_parts(gate_act)
    slot_grads = recv_grads.reshape(-1, feature_width)
    weight_wide = recv_scale.reshape(-1).astype(jnp.float32)[:, None]
    into_hidden = contract_last(slot_grads, down_piece)
    route_terms = jnp.sum(into_hidden * hidden.astype(jnp.float32), axis=1).astype(jnp.bfloat16)
    hidden_grad = weight_wide * into_hidden
    gate_grad = (hidden_grad * up_act * silu_slope).astype(jnp.bfloat16)
    up_grad = (hidden_grad * active).astype(jnp.bfloat16)
    row_grad = (
        jnp.dot(gate_grad, gate_piece, preferred_element_type=jnp.float32)
        + jnp.dot(up_grad, up_piece, preferred_element_type=jnp.float32)
    ).astype(jnp.bfloat16)
    scaled_grad = (weight_wide * slot_grads.astype(jnp.float32)).astype(jnp.bfloat16)
    grad_gate = contract_first(gate_grad, slot_rows).astype(jnp.bfloat16)[None]
    grad_up = contract_first(up_grad, slot_rows).astype(jnp.bfloat16)[None]
    grad_down = contract_first(hidden, scaled_grad).astype(jnp.bfloat16)[None]
    back_rows, back_terms = (
        lax.all_to_all(
            row_grad.reshape(data_size, capacity, feature_width),
            "dp",
            split_axis=0,
            concat_axis=0,
            tiled=True,
        ),
        lax.all_to_all(
            route_terms.reshape(data_size, capacity), "dp", split_axis=0, concat_axis=0, tiled=True
        ),
    )
    token_sum = jnp.dot(
        token_place, back_rows.reshape(-1, feature_width), preferred_element_type=jnp.float32
    )
    row_place = (
        (wide_row[None, :] == jnp.arange(row_count, dtype=jnp.int32)[:, None])
        & (wide_live[None, :] > 0)
    ).astype(jnp.bfloat16)
    route_sum = jnp.dot(
        row_place, back_terms.reshape(-1), preferred_element_type=jnp.float32
    ).reshape(tok_local, topk_count)
    mixed_part, token_part, route_part = (
        lax.psum_scatter(mixed_sum, "expert", scatter_dimension=1, tiled=True),
        lax.psum_scatter(token_sum, "expert", scatter_dimension=1, tiled=True),
        lax.psum_scatter(route_sum, "expert", scatter_dimension=0, tiled=True),
    )
    return (
        mixed_part.astype(jnp.bfloat16),
        token_part.astype(jnp.bfloat16),
        route_part,
        grad_gate,
        grad_up,
        grad_down,
    )


MESH = pl.DeviceIdType.MESH
GATHER_ORDER = (0, 1, 3, 2)
SCATTER_ORDER = (2, 1, 3, 0)


def remote(src, dst, sems, index, device):
    return pltpu.make_async_remote_copy(
        src_ref=src,
        dst_ref=dst,
        send_sem=sems.at[(0,) + index],
        recv_sem=sems.at[(1,) + index],
        device_id=device,
        device_id_type=MESH,
    )


def dense_kernel(
    tok_ref, rw_ref, ids_ref, wg_ref, wu_ref, wd_ref, gy_ref,
    mixed_ref, token_ref, route_ref, gg_ref, gu_ref, gd_ref,
    acts, parts, weights, wide, names_wide, gate, up, into, hw, gg, ug, turned,
    half_in, full_in, z_out, z_in, z_own, route, route_in, route_sum, route_z, wg_out, wg_in,
    s_z, s_plane, s_fwd, s_wide, s_wt, s_local, s_r1, s_r2, s_r3, s_rt, s_rz, s_wg,
):
    f32, bf16 = jnp.float32, jnp.bfloat16
    rows, feat = tok_ref.shape
    unit = wg_ref.shape[1]
    topk = ids_ref.shape[0]
    half = rows // 2
    quarters = acts.shape[1]
    d, z = lax.axis_index("dp"), lax.axis_index("expert")
    core, x, y = lax.rem(d, 2), lax.rem(d // 2, 2), d // 4
    x_dev = (y * 4 + (1 - x) * 2 + core, z)
    y_dev = ((1 - y) * 4 + x * 2 + core, z)
    diag_dev = ((1 - y) * 4 + (1 - x) * 2 + core, z)
    twin = (y * 4 + x * 2 + (1 - core), z)
    expert = z * (lax.axis_size("dp") // PIECES) + d // PIECES

    def quarter(r):
        return lax.rem(z + r, quarters)

    def z_dev(r):
        return (d, quarter(r))

    barrier = pltpu.get_barrier_semaphore()
    others = [x_dev, y_dev, diag_dev, twin] + [z_dev(r) for r in range(1, quarters)]
    for dev in others:
        pl.semaphore_signal(barrier, inc=1, device_id=dev, device_id_type=MESH)
    pl.semaphore_wait(barrier, len(others))

    own, at_x, at_y, at_d = (pl.ds(i * rows, rows) for i in range(4))
    d_top, d_low = pl.ds(3 * rows, half), pl.ds(3 * rows + half, half)
    x_top, x_low = pl.ds(rows, half), pl.ds(rows + half, half)
    y_top, y_low = pl.ds(2 * rows, half), pl.ds(2 * rows + half, half)
    started = []

    def go(copy):
        copy.start()
        started.append(copy)

    def z_send(a, s):
        return remote((tok_ref, gy_ref)[a], acts.at[a, z, own], s_z, (a, quarters - 1 - s), z_dev(s))

    def z_arrive(a, r):
        block = acts.at[a, quarter(r), own]
        remote(block, block, s_z, (a, r - 1), z_dev(r)).wait_recv()

    def plane(a, r):
        q = quarter(r)
        src = (tok_ref, gy_ref)[a] if r == 0 else acts.at[a, q, own]
        return (
            remote(src, acts.at[a, q, at_x], s_plane, (a, 0, r), x_dev),
            remote(src, acts.at[a, q, at_y], s_plane, (a, 1, r), y_dev),
        )

    def forward(a, r):
        q = quarter(r)
        return (
            remote(acts.at[a, q, x_top], acts.at[a, q, d_top], s_fwd, (a, 0, r), y_dev),
            remote(acts.at[a, q, y_low], acts.at[a, q, d_low], s_fwd, (a, 1, r), x_dev),
        )

    def send_plane(a, r):
        for copy in plane(a, r):
            go(copy)

    def pass_on(a, r):
        for arrived, onward in zip(plane(a, r), forward(a, r)):
            arrived.wait_recv()
            go(onward)

    def complete(a, r):
        for copy in forward(a, r):
            copy.wait_recv()

    for s in (1, 3, 2):
        go(z_send(0, s))
    send_plane(0, 0)
    send_plane(1, 0)
    local, lent = [], []
    for a, ref in enumerate((tok_ref, gy_ref)):
        local.append(pltpu.make_async_copy(ref, acts.at[a, z, own], s_local.at[3 + a]))
        local[a].start()
    for m, ref in enumerate((wg_ref, wu_ref, wd_ref)):
        copy = pltpu.make_async_copy(ref.at[0], weights.at[m, pl.ds(0, unit)], s_local.at[m])
        copy.start()
        local.append(copy)
        lent.append(remote(ref.at[0], weights.at[m, pl.ds(unit, unit)], s_wt, (m,), twin))
        go(lent[m])

    lane = lax.broadcasted_iota(jnp.int32, (rows, 128), 1)
    ids, rw = ids_ref[...], rw_ref[...].astype(f32)
    level = lax.broadcasted_iota(jnp.int32, (128, rows), 0)
    spread, named = jnp.zeros((128, rows), f32), jnp.zeros((128, rows), f32)
    for k in range(topk):
        spread = spread + jnp.where(level == ids[k : k + 1, :], rw[k : k + 1, :], 0.0)
        named = named + jnp.where(level == k, ids[k : k + 1, :].astype(f32), 0.0)
    wide[own, :] = spread.T
    names_wide[...] = named.T
    wide_copies = [
        remote(wide.at[own], wide.at[place], s_wide, (i,), dev)
        for i, (place, dev) in enumerate(((at_x, x_dev), (at_y, y_dev), (at_d, diag_dev)))
    ]
    for copy in wide_copies:
        go(copy)
    for i, r in enumerate(GATHER_ORDER[1:]):
        z_arrive(0, r)
        send_plane(0, r)
        if i < 2:
            pass_on(i, 0)
    for s in (1, 3, 2):
        go(z_send(1, s))
    for copy in local:
        copy.wait()
    for copy in lent:
        copy.wait_recv()

    def columns(q):
        return pl.ds(pl.multiple_of(q * feat, feat), feat)

    def add_forward(i, r):
        q = quarter(r)
        for total, m in ((gate, 0), (up, 1)):
            term = contract_last(acts[0, q], weights[m, :, columns(q)])
            total[...] = term if i == 0 else total[...] + term

    for i, r in enumerate(GATHER_ORDER):
        if i > 0:
            pass_on(0, r)
            z_arrive(1, r)
            send_plane(1, r)
            complete(0, GATHER_ORDER[i - 1])
            add_forward(i - 1, GATHER_ORDER[i - 1])
    complete(0, GATHER_ORDER[-1])
    add_forward(len(GATHER_ORDER) - 1, GATHER_ORDER[-1])
    for copy in wide_copies:
        copy.wait_recv()

    def block_rows(b):
        return pl.ds(pl.multiple_of(b * rows, rows), rows)

    def scale_of(b):
        return jnp.sum(jnp.where(lane == expert, wide[block_rows(b), :], 0.0), axis=1, keepdims=True)

    @pl.loop(0, 4)
    def _(b):
        at = block_rows(b)
        active, _slope = silu_parts(gate[at, :])
        weighted = scale_of(b) * (active * up[at, :])
        hw[at, :] = weighted.astype(bf16)
        turned[2, :, at] = weighted.T.astype(bf16)

    def first(a, r):
        q = quarter(r)
        return (
            remote(parts.at[a, q, d_top], half_in.at[a, 0, r], s_r1, (a, 0, r), x_dev),
            remote(parts.at[a, q, d_low], half_in.at[a, 1, r], s_r1, (a, 1, r), y_dev),
        )

    def second(a, r):
        q = quarter(r)
        return (
            remote(parts.at[a, q, at_x], full_in.at[a, 0, r], s_r2, (a, 0, r), x_dev),
            remote(parts.at[a, q, at_y], full_in.at[a, 1, r], s_r2, (a, 1, r), y_dev),
        )

    def send_first(a, r):
        for copy in first(a, r):
            go(copy)

    def add_first(a, r):
        q = quarter(r)
        for i, (copy, place) in enumerate(zip(first(a, r), (y_top, x_low))):
            copy.wait_recv()
            here = parts[a, q, place, :].astype(f32) + half_in[a, i, r].astype(f32)
            parts[a, q, place, :] = here.astype(bf16)
        for copy in second(a, r):
            go(copy)

    def third(a, r):
        return remote(z_out.at[a, r - 1], z_in.at[a, quarters - 1 - r], s_r3, (a, quarters - 1 - r), z_dev(r))

    def add_second(a, r):
        for copy in second(a, r):
            copy.wait_recv()
        total = parts[a, quarter(r), own, :].astype(f32)
        total = total + full_in[a, 0, r].astype(f32) + full_in[a, 1, r].astype(f32)
        if r == 0:
            z_own[a] = total
        else:
            z_out[a, r - 1] = total.astype(bf16)
            go(third(a, r))

    def finish(a, out_ref):
        total = z_own[a]
        for r in range(1, quarters):
            slot = z_in.at[a, r - 1]
            remote(slot, slot, s_r3, (a, r - 1), z_dev(r)).wait_recv()
            total = total + z_in[a, r - 1].astype(f32)
        out_ref[...] = total.astype(bf16)

    for near, r in zip(GATHER_ORDER, SCATTER_ORDER):
        q = quarter(r)
        if near > 0:
            pass_on(1, near)
        parts[0, q] = jnp.dot(
            hw[...], weights[2, :, columns(q)], preferred_element_type=f32
        ).astype(bf16)
        send_first(0, r)

    for i, (near, r) in enumerate(zip(GATHER_ORDER, SCATTER_ORDER)):
        q = quarter(near)
        complete(1, near)
        term = contract_last(acts[1, q], weights[2, :, columns(q)])
        into[...] = term if i == 0 else into[...] + term
        add_first(0, r)

    @pl.loop(0, 4)
    def _(b):
        at = block_rows(b)
        gate_act, up_act, back = gate[at, :], up[at, :], into[at, :]
        active, slope = silu_parts(gate_act)
        term = jnp.sum(back * (active * up_act), axis=1, keepdims=True)
        route[at, :] = jnp.where(lane == expert, term, 0.0)
        scaled = scale_of(b) * back
        gate_grad, up_grad = scaled * up_act * slope, scaled * active
        gg[at, :] = gate_grad.astype(bf16)
        ug[at, :] = up_grad.astype(bf16)
        turned[0, :, at] = gate_grad.T.astype(bf16)
        turned[1, :, at] = up_grad.T.astype(bf16)

    for r in SCATTER_ORDER:
        q = quarter(r)
        total = jnp.dot(gg[...], weights[0, :, columns(q)], preferred_element_type=f32)
        total = total + jnp.dot(ug[...], weights[1, :, columns(q)], preferred_element_type=f32)
        parts[1, q] = total.astype(bf16)
        send_first(1, r)
    for r in SCATTER_ORDER:
        add_second(0, r)

    route_copies = [
        remote(route.at[place], route_in.at[i], s_rt, (i,), dev)
        for i, (place, dev) in enumerate(((at_x, x_dev), (at_y, y_dev), (at_d, diag_dev)))
    ]
    for copy in route_copies:
        go(copy)

    lent_grads = []
    for m in range(3):
        @pl.loop(0, quarters)
        def _(q, m=m):
            wg_out[m, :, columns(q)] = jnp.dot(
                turned[m, pl.ds(unit, unit), :], acts[m // 2, q], preferred_element_type=f32
            ).astype(bf16)

        lent_grads.append(remote(wg_out.at[m], wg_in.at[m], s_wg, (m,), twin))
        go(lent_grads[m])

    for r in SCATTER_ORDER:
        add_first(1, r)

    for copy in route_copies:
        copy.wait_recv()
    route_sum[...] = route[own, :] + route_in[0] + route_in[1] + route_in[2]
    slab = rows // quarters

    def slab_of(q):
        return pl.ds(pl.multiple_of(q * slab, slab), slab)

    slab_copies = []
    for s in range(1, quarters):
        slab_copies.append(remote(route_sum.at[slab_of(quarter(s))], route_z.at[quarters - 1 - s], s_rz, (quarters - 1 - s,), z_dev(s)))
        slab_copies[-1].start()

    for m, out_ref in enumerate((gg_ref, gu_ref, gd_ref)):
        lent_grads[m].wait_recv()

        @pl.loop(0, quarters)
        def _(q, m=m, out_ref=out_ref):
            total = jnp.dot(turned[m, pl.ds(0, unit), :], acts[m // 2, q], preferred_element_type=f32)
            out_ref[0, :, columns(q)] = (total + wg_in[m, :, columns(q)].astype(f32)).astype(bf16)

    finish(0, mixed_ref)
    for r in SCATTER_ORDER:
        add_second(1, r)

    total = route_sum[slab_of(z), :]
    for r in range(1, quarters):
        slot = route_z.at[r - 1]
        remote(slot, slot, s_rz, (r - 1,), z_dev(r)).wait_recv()
        total = total + route_z[r - 1]
    for copy in slab_copies:
        copy.wait_send()
    names = names_wide[slab_of(z), :]
    lane_slab = lax.broadcasted_iota(jnp.int32, (slab, 128), 1)
    picked = jnp.zeros((slab, 128), f32)
    for k in range(topk):
        match = lane_slab.astype(f32) == names[:, k : k + 1]
        value = jnp.sum(jnp.where(match, total, 0.0), axis=1, keepdims=True)
        picked = jnp.where(lane_slab == k, value, picked)
    route_sum[pl.ds(0, slab), :] = picked
    route_ref[...] = route_sum[...].T[:topk, :slab]
    finish(1, token_ref)
    for copy in started:
        copy.wait_send()


def deliver(*refs):
    sems = refs[-1]
    count = len(refs) // 2
    copies = [pltpu.make_async_copy(refs[i], refs[count + i], sems.at[i]) for i in range(count)]
    for copy in copies:
        copy.start()
    for copy in copies:
        copy.wait()


def dense_device(tokens, route_weight, expert_ids, gate_weight, up_weight, down_weight, grad_output):
    quarters = lax.axis_size("expert")
    rows, feat = tokens.shape
    unit, width = gate_weight.shape[1:]
    topk = expert_ids.shape[1]
    f32, bf16 = jnp.float32, jnp.bfloat16
    vmem = pl.BlockSpec(memory_space=pltpu.VMEM)
    hbm = pl.BlockSpec(memory_space=pl.ANY)
    stay = pl.BlockSpec(memory_space=pltpu.HBM)
    every, both, half = 4 * rows, 2 * unit, rows // 2
    dma = pltpu.SemaphoreType.DMA
    grads = jax.ShapeDtypeStruct((1, unit, width), bf16)
    results = pl.pallas_call(
        dense_kernel,
        out_shape=(
            jax.ShapeDtypeStruct((rows, feat), bf16),
            jax.ShapeDtypeStruct((rows, feat), bf16),
            jax.ShapeDtypeStruct((topk, rows // quarters), f32),
            grads,
            grads,
            grads,
        ),
        in_specs=[stay, vmem, vmem, stay, stay, stay, stay],
        out_specs=(vmem,) * 6,
        scratch_shapes=[
            pltpu.VMEM((2, quarters, every, feat), bf16),
            pltpu.VMEM((2, quarters, every, feat), bf16),
            pltpu.VMEM((3, both, width), bf16),
            pltpu.VMEM((every, 128), f32),
            pltpu.VMEM((rows, 128), f32),
            pltpu.VMEM((every, both), f32),
            pltpu.VMEM((every, both), f32),
            pltpu.VMEM((every, both), f32),
            pltpu.VMEM((every, both), bf16),
            pltpu.VMEM((every, both), bf16),
            pltpu.VMEM((every, both), bf16),
            pltpu.VMEM((3, both, every), bf16),
            pltpu.VMEM((2, 2, quarters, half, feat), bf16),
            pltpu.VMEM((2, 2, quarters, rows, feat), bf16),
            pltpu.VMEM((2, quarters - 1, rows, feat), bf16),
            pltpu.VMEM((2, quarters - 1, rows, feat), bf16),
            pltpu.VMEM((2, rows, feat), f32),
            pltpu.VMEM((every, 128), f32),
            pltpu.VMEM((3, rows, 128), f32),
            pltpu.VMEM((rows, 128), f32),
            pltpu.VMEM((quarters - 1, rows // quarters, 128), f32),
            pltpu.VMEM((3, unit, width), bf16),
            pltpu.VMEM((3, unit, width), bf16),
            dma((2, 2, quarters - 1)),
            dma((2, 2, 2, quarters)),
            dma((2, 2, 2, quarters)),
            dma((2, 3)),
            dma((2, 3)),
            dma((5,)),
            dma((2, 2, 2, quarters)),
            dma((2, 2, 2, quarters)),
            dma((2, 2, quarters - 1)),
            dma((2, 3)),
            dma((2, quarters - 1)),
            dma((2, 3)),
        ],
        compiler_params=pltpu.CompilerParams(
            collective_id=0, has_side_effects=True, vmem_limit_bytes=51 * 2**20
        ),
        cost_estimate=pl.CostEstimate(
            flops=18 * every * both * width, bytes_accessed=12 * unit * width, transcendentals=2 * every * both
        ),
    )(tokens, route_weight.T, expert_ids.T, gate_weight, up_weight, down_weight, grad_output)
    count = len(results)
    mixed, token_part, route_part, *weight_grads = pl.pallas_call(
        deliver,
        out_shape=tuple(jax.ShapeDtypeStruct(v.shape, v.dtype) for v in results),
        in_specs=[hbm] * count,
        out_specs=(hbm,) * count,
        scratch_shapes=[dma((count,))],
    )(*results)
    return (mixed, token_part, route_part.T, *weight_grads)


def on_device(tokens, route_weight, expert_ids, *rest):
    shape = (lax.axis_size("dp"), lax.axis_size("expert"))
    experts = shape[0] // PIECES * shape[1]
    dense = shape == (8, 4) and experts == expert_ids.shape[1]
    body = dense_device if dense else slot_device
    return body(tokens, route_weight, expert_ids, *rest)


def solution(mesh):
    return jax.shard_map(
        on_device,
        mesh=mesh,
        in_specs=(
            P("dp", "expert"),
            P("dp", None),
            P("dp", None),
            P("expert", "dp", None),
            P("expert", "dp", None),
            P("expert", "dp", None),
            P("dp", "expert"),
        ),
        out_specs=(
            P("dp", "expert"),
            P("dp", "expert"),
            P(("dp", "expert"), None),
            P("expert", "dp", None),
            P("expert", "dp", None),
            P("expert", "dp", None),
        ),
        check_vma=False,
    )
```

```python
import jax
import jax.numpy as jnp
from jax import lax
from jax.experimental import pallas as pl
from jax.experimental.pallas import tpu as pltpu
from jax.sharding import PartitionSpec as P

PIECES = 4


def contract_last(left_side, right_side):
    return lax.dot_general(
        left_side, right_side, (((1,), (1,)), ((), ())), preferred_element_type=jnp.float32
    )


def contract_first(left_side, right_side):
    return lax.dot_general(
        left_side, right_side, (((0,), (0,)), ((), ())), preferred_element_type=jnp.float32
    )


def silu_parts(gate_act):
    sigmoid_val = jax.nn.sigmoid(gate_act)
    return (gate_act * sigmoid_val, sigmoid_val * (1.0 + gate_act * (1.0 - sigmoid_val)))


def expert_forward(slot_rows, slot_scale, gate_piece, up_piece, down_piece):
    gate_act = contract_last(slot_rows, gate_piece)
    up_act = contract_last(slot_rows, up_piece)
    active, silu_slope = silu_parts(gate_act)
    hidden = (active * up_act).astype(jnp.bfloat16)
    partial_out = jnp.dot(hidden, down_piece, preferred_element_type=jnp.float32)
    scaled = (slot_scale.astype(jnp.float32)[:, None] * partial_out).astype(jnp.bfloat16)
    return (scaled, gate_act, up_act, hidden)


def slot_device(tokens, route_weight, expert_ids, gate_weight, up_weight, down_weight, grad_output):
    groups = lax.axis_size("expert")
    group_index = lax.axis_index("expert")
    data_size = lax.axis_size("dp")
    exp_local = data_size // PIECES
    tok_local, topk_count = expert_ids.shape
    capacity = min(tok_local, 2 * tok_local * topk_count // (exp_local * groups))
    full_tokens, full_grad = (
        lax.all_gather(tokens, "expert", axis=1, tiled=True),
        lax.all_gather(grad_output, "expert", axis=1, tiled=True),
    )
    feature_width = full_tokens.shape[1]
    gate_piece = gate_weight[0]
    up_piece = up_weight[0]
    down_piece = down_weight[0]
    flat_ids = expert_ids.reshape(-1)
    row_count = flat_ids.shape[0]
    owned_rows = flat_ids // exp_local == group_index
    local_ids = flat_ids % exp_local
    chosen = (
        (local_ids[:, None] == jnp.arange(exp_local, dtype=jnp.int32)[None, :])
        & owned_rows[:, None]
    ).astype(jnp.int32)
    slot_ranks = jnp.sum(chosen * (jnp.cumsum(chosen, axis=0) - 1), axis=1)
    slot_count = exp_local * capacity
    slot_pos = jnp.where(owned_rows, local_ids * capacity + slot_ranks, slot_count)
    row_index = jnp.arange(row_count, dtype=jnp.int32)
    row_of = jnp.zeros((slot_count,), jnp.int32).at[slot_pos].set(row_index, mode="drop")
    slot_live = (
        jnp.zeros((slot_count,), jnp.int32).at[slot_pos].set(jnp.ones_like(row_index), mode="drop")
    )
    token_of = row_of // topk_count
    keep_mask = slot_live.astype(tokens.dtype)[:, None]
    slot_weight = route_weight.reshape(-1)[row_of] * slot_live.astype(route_weight.dtype)

    def spread(values):
        trailing = values.shape[1:]
        grouped = values.reshape((exp_local, 1, capacity) + trailing)
        return jnp.broadcast_to(grouped, (exp_local, PIECES, capacity) + trailing).reshape(
            (data_size, capacity) + trailing
        )

    send_rows = spread(full_tokens[token_of] * keep_mask)
    send_weight = spread(slot_weight)
    send_grads = spread(full_grad[token_of] * keep_mask)
    recv_grads = None
    recv_scale = None
    recv_rows, recv_weight = (
        lax.all_to_all(send_rows, "dp", split_axis=0, concat_axis=0, tiled=True),
        lax.all_to_all(send_weight, "dp", split_axis=0, concat_axis=0, tiled=True),
    )
    scaled, gate_act, up_act, hidden = expert_forward(
        recv_rows.reshape(-1, feature_width),
        recv_weight.reshape(-1),
        gate_piece,
        up_piece,
        down_piece,
    )
    returned = lax.all_to_all(
        scaled.reshape(data_size, capacity, feature_width),
        "dp",
        split_axis=0,
        concat_axis=0,
        tiled=True,
    )
    slot_rows = recv_rows.reshape(-1, feature_width)
    wide_token = spread(token_of).reshape(-1)
    wide_live = spread(slot_live).reshape(-1)
    wide_row = spread(row_of).reshape(-1)
    token_place = (
        (wide_token[None, :] == jnp.arange(tok_local, dtype=jnp.int32)[:, None])
        & (wide_live[None, :] > 0)
    ).astype(jnp.bfloat16)
    mixed_sum = jnp.dot(
        token_place, returned.reshape(-1, feature_width), preferred_element_type=jnp.float32
    )
    recv_grads, recv_scale = (
        lax.all_to_all(send_grads, "dp", split_axis=0, concat_axis=0, tiled=True),
        lax.all_to_all(send_weight, "dp", split_axis=0, concat_axis=0, tiled=True),
    )
    active, silu_slope = silu_parts(gate_act)
    slot_grads = recv_grads.reshape(-1, feature_width)
    weight_wide = recv_scale.reshape(-1).astype(jnp.float32)[:, None]
    into_hidden = contract_last(slot_grads, down_piece)
    route_terms = jnp.sum(into_hidden * hidden.astype(jnp.float32), axis=1).astype(jnp.bfloat16)
    hidden_grad = weight_wide * into_hidden
    gate_grad = (hidden_grad * up_act * silu_slope).astype(jnp.bfloat16)
    up_grad = (hidden_grad * active).astype(jnp.bfloat16)
    row_grad = (
        jnp.dot(gate_grad, gate_piece, preferred_element_type=jnp.float32)
        + jnp.dot(up_grad, up_piece, preferred_element_type=jnp.float32)
    ).astype(jnp.bfloat16)
    scaled_grad = (weight_wide * slot_grads.astype(jnp.float32)).astype(jnp.bfloat16)
    grad_gate = contract_first(gate_grad, slot_rows).astype(jnp.bfloat16)[None]
    grad_up = contract_first(up_grad, slot_rows).astype(jnp.bfloat16)[None]
    grad_down = contract_first(hidden, scaled_grad).astype(jnp.bfloat16)[None]
    back_rows, back_terms = (
        lax.all_to_all(
            row_grad.reshape(data_size, capacity, feature_width),
            "dp",
            split_axis=0,
            concat_axis=0,
            tiled=True,
        ),
        lax.all_to_all(
            route_terms.reshape(data_size, capacity), "dp", split_axis=0, concat_axis=0, tiled=True
        ),
    )
    token_sum = jnp.dot(
        token_place, back_rows.reshape(-1, feature_width), preferred_element_type=jnp.float32
    )
    row_place = (
        (wide_row[None, :] == jnp.arange(row_count, dtype=jnp.int32)[:, None])
        & (wide_live[None, :] > 0)
    ).astype(jnp.bfloat16)
    route_sum = jnp.dot(
        row_place, back_terms.reshape(-1), preferred_element_type=jnp.float32
    ).reshape(tok_local, topk_count)
    mixed_part, token_part, route_part = (
        lax.psum_scatter(mixed_sum, "expert", scatter_dimension=1, tiled=True),
        lax.psum_scatter(token_sum, "expert", scatter_dimension=1, tiled=True),
        lax.psum_scatter(route_sum, "expert", scatter_dimension=0, tiled=True),
    )
    return (
        mixed_part.astype(jnp.bfloat16),
        token_part.astype(jnp.bfloat16),
        route_part,
        grad_gate,
        grad_up,
        grad_down,
    )


MESH = pl.DeviceIdType.MESH
GATHER_ORDER = (0, 1, 3, 2)
SCATTER_ORDER = (2, 1, 3, 0)


def remote(src, dst, sems, index, device):
    return pltpu.make_async_remote_copy(
        src_ref=src,
        dst_ref=dst,
        send_sem=sems.at[(0,) + index],
        recv_sem=sems.at[(1,) + index],
        device_id=device,
        device_id_type=MESH,
    )


def dense_kernel(
    tok_ref, rw_ref, ids_ref, wg_ref, wu_ref, wd_ref, gy_ref,
    mixed_ref, token_ref, route_ref, gg_ref, gu_ref, gd_ref,
    acts, parts, weights, wide, names_wide, gate, up, into, hw, gg, ug, turned,
    half_in, full_in, z_out, z_in, z_own, route, route_in, route_sum, route_z, wg_out, wg_in,
    s_z, s_plane, s_fwd, s_wide, s_wt, s_local, s_r1, s_r2, s_r3, s_rt, s_rz, s_wg,
):
    f32, bf16 = jnp.float32, jnp.bfloat16
    rows, feat = tok_ref.shape
    unit = wg_ref.shape[1]
    topk = ids_ref.shape[0]
    half = rows // 2
    quarters = acts.shape[1]
    d, z = lax.axis_index("dp"), lax.axis_index("expert")
    core, x, y = lax.rem(d, 2), lax.rem(d // 2, 2), d // 4
    x_dev = (y * 4 + (1 - x) * 2 + core, z)
    y_dev = ((1 - y) * 4 + x * 2 + core, z)
    diag_dev = ((1 - y) * 4 + (1 - x) * 2 + core, z)
    twin = (y * 4 + x * 2 + (1 - core), z)
    expert = z * (lax.axis_size("dp") // PIECES) + d // PIECES

    def quarter(r):
        return lax.rem(z + r, quarters)

    def z_dev(r):
        return (d, quarter(r))

    barrier = pltpu.get_barrier_semaphore()
    others = [x_dev, y_dev, diag_dev, twin] + [z_dev(r) for r in range(1, quarters)]
    for dev in others:
        pl.semaphore_signal(barrier, inc=1, device_id=dev, device_id_type=MESH)
    pl.semaphore_wait(barrier, len(others))

    own, at_x, at_y, at_d = (pl.ds(i * rows, rows) for i in range(4))
    d_top, d_low = pl.ds(3 * rows, half), pl.ds(3 * rows + half, half)
    x_top, x_low = pl.ds(rows, half), pl.ds(rows + half, half)
    y_top, y_low = pl.ds(2 * rows, half), pl.ds(2 * rows + half, half)
    started = []

    def go(copy):
        copy.start()
        started.append(copy)

    def z_send(a, s):
        return remote((tok_ref, gy_ref)[a], acts.at[a, z, own], s_z, (a, quarters - 1 - s), z_dev(s))

    def z_arrive(a, r):
        block = acts.at[a, quarter(r), own]
        remote(block, block, s_z, (a, r - 1), z_dev(r)).wait_recv()

    def plane(a, r):
        q = quarter(r)
        src = (tok_ref, gy_ref)[a] if r == 0 else acts.at[a, q, own]
        return (
            remote(src, acts.at[a, q, at_x], s_plane, (a, 0, r), x_dev),
            remote(src, acts.at[a, q, at_y], s_plane, (a, 1, r), y_dev),
        )

    def forward(a, r):
        q = quarter(r)
        return (
            remote(acts.at[a, q, x_top], acts.at[a, q, d_top], s_fwd, (a, 0, r), y_dev),
            remote(acts.at[a, q, y_low], acts.at[a, q, d_low], s_fwd, (a, 1, r), x_dev),
        )

    def send_plane(a, r):
        for copy in plane(a, r):
            go(copy)

    def pass_on(a, r):
        for arrived, onward in zip(plane(a, r), forward(a, r)):
            arrived.wait_recv()
            go(onward)

    def complete(a, r):
        for copy in forward(a, r):
            copy.wait_recv()

    for s in (1, 3, 2):
        go(z_send(0, s))
    send_plane(0, 0)
    send_plane(1, 0)
    local, lent = [], []
    for a, ref in enumerate((tok_ref, gy_ref)):
        local.append(pltpu.make_async_copy(ref, acts.at[a, z, own], s_local.at[3 + a]))
        local[a].start()
    for m, ref in enumerate((wg_ref, wu_ref, wd_ref)):
        copy = pltpu.make_async_copy(ref.at[0], weights.at[m, pl.ds(0, unit)], s_local.at[m])
        copy.start()
        local.append(copy)
        lent.append(remote(ref.at[0], weights.at[m, pl.ds(unit, unit)], s_wt, (m,), twin))
        go(lent[m])

    lane = lax.broadcasted_iota(jnp.int32, (rows, 128), 1)
    ids, rw = ids_ref[...], rw_ref[...].astype(f32)
    level = lax.broadcasted_iota(jnp.int32, (128, rows), 0)
    spread, named = jnp.zeros((128, rows), f32), jnp.zeros((128, rows), f32)
    for k in range(topk):
        spread = spread + jnp.where(level == ids[k : k + 1, :], rw[k : k + 1, :], 0.0)
        named = named + jnp.where(level == k, ids[k : k + 1, :].astype(f32), 0.0)
    wide[own, :] = spread.T
    names_wide[...] = named.T
    wide_copies = [
        remote(wide.at[own], wide.at[place], s_wide, (i,), dev)
        for i, (place, dev) in enumerate(((at_x, x_dev), (at_y, y_dev), (at_d, diag_dev)))
    ]
    for copy in wide_copies:
        go(copy)
    for i, r in enumerate(GATHER_ORDER[1:]):
        z_arrive(0, r)
        send_plane(0, r)
        if i < 2:
            pass_on(i, 0)
    for s in (1, 3, 2):
        go(z_send(1, s))
    for copy in local:
        copy.wait()
    for copy in lent:
        copy.wait_recv()

    def columns(q):
        return pl.ds(pl.multiple_of(q * feat, feat), feat)

    def add_forward(i, r):
        q = quarter(r)
        for total, m in ((gate, 0), (up, 1)):
            term = contract_last(acts[0, q], weights[m, :, columns(q)])
            total[...] = term if i == 0 else total[...] + term

    for i, r in enumerate(GATHER_ORDER):
        if i > 0:
            pass_on(0, r)
            z_arrive(1, r)
            send_plane(1, r)
            complete(0, GATHER_ORDER[i - 1])
            add_forward(i - 1, GATHER_ORDER[i - 1])
    complete(0, GATHER_ORDER[-1])
    add_forward(len(GATHER_ORDER) - 1, GATHER_ORDER[-1])
    for copy in wide_copies:
        copy.wait_recv()

    def block_rows(b):
        return pl.ds(pl.multiple_of(b * rows, rows), rows)

    def scale_of(b):
        return jnp.sum(jnp.where(lane == expert, wide[block_rows(b), :], 0.0), axis=1, keepdims=True)

    @pl.loop(0, 4)
    def _(b):
        at = block_rows(b)
        active, _slope = silu_parts(gate[at, :])
        weighted = scale_of(b) * (active * up[at, :])
        hw[at, :] = weighted.astype(bf16)
        turned[2, :, at] = weighted.T.astype(bf16)

    def first(a, r):
        q = quarter(r)
        return (
            remote(parts.at[a, q, d_top], half_in.at[a, 0, r], s_r1, (a, 0, r), x_dev),
            remote(parts.at[a, q, d_low], half_in.at[a, 1, r], s_r1, (a, 1, r), y_dev),
        )

    def second(a, r):
        q = quarter(r)
        return (
            remote(parts.at[a, q, at_x], full_in.at[a, 0, r], s_r2, (a, 0, r), x_dev),
            remote(parts.at[a, q, at_y], full_in.at[a, 1, r], s_r2, (a, 1, r), y_dev),
        )

    def send_first(a, r):
        for copy in first(a, r):
            go(copy)

    def add_first(a, r):
        q = quarter(r)
        for i, (copy, place) in enumerate(zip(first(a, r), (y_top, x_low))):
            copy.wait_recv()
            here = parts[a, q, place, :].astype(f32) + half_in[a, i, r].astype(f32)
            parts[a, q, place, :] = here.astype(bf16)
        for copy in second(a, r):
            go(copy)

    def third(a, r):
        return remote(z_out.at[a, r - 1], z_in.at[a, quarters - 1 - r], s_r3, (a, quarters - 1 - r), z_dev(r))

    def add_second(a, r):
        for copy in second(a, r):
            copy.wait_recv()
        total = parts[a, quarter(r), own, :].astype(f32)
        total = total + full_in[a, 0, r].astype(f32) + full_in[a, 1, r].astype(f32)
        if r == 0:
            z_own[a] = total
        else:
            z_out[a, r - 1] = total.astype(bf16)
            go(third(a, r))

    def finish(a, out_ref):
        total = z_own[a]
        for r in range(1, quarters):
            slot = z_in.at[a, r - 1]
            remote(slot, slot, s_r3, (a, r - 1), z_dev(r)).wait_recv()
            total = total + z_in[a, r - 1].astype(f32)
        out_ref[...] = total.astype(bf16)

    for near, r in zip(GATHER_ORDER, SCATTER_ORDER):
        q = quarter(r)
        if near > 0:
            pass_on(1, near)
        parts[0, q] = jnp.dot(
            hw[...], weights[2, :, columns(q)], preferred_element_type=f32
        ).astype(bf16)
        send_first(0, r)

    for i, (near, r) in enumerate(zip(GATHER_ORDER, SCATTER_ORDER)):
        q = quarter(near)
        complete(1, near)
        term = contract_last(acts[1, q], weights[2, :, columns(q)])
        into[...] = term if i == 0 else into[...] + term
        add_first(0, r)

    @pl.loop(0, 4)
    def _(b):
        at = block_rows(b)
        gate_act, up_act, back = gate[at, :], up[at, :], into[at, :]
        active, slope = silu_parts(gate_act)
        term = jnp.sum(back * (active * up_act), axis=1, keepdims=True)
        route[at, :] = jnp.where(lane == expert, term, 0.0)
        scaled = scale_of(b) * back
        gate_grad, up_grad = scaled * up_act * slope, scaled * active
        gg[at, :] = gate_grad.astype(bf16)
        ug[at, :] = up_grad.astype(bf16)
        turned[0, :, at] = gate_grad.T.astype(bf16)
        turned[1, :, at] = up_grad.T.astype(bf16)

    for r in SCATTER_ORDER:
        q = quarter(r)
        total = jnp.dot(gg[...], weights[0, :, columns(q)], preferred_element_type=f32)
        total = total + jnp.dot(ug[...], weights[1, :, columns(q)], preferred_element_type=f32)
        parts[1, q] = total.astype(bf16)
        send_first(1, r)
    route_copies = [
        remote(route.at[place], route_in.at[i], s_rt, (i,), dev)
        for i, (place, dev) in enumerate(((at_x, x_dev), (at_y, y_dev), (at_d, diag_dev)))
    ]
    for copy in route_copies:
        go(copy)

    lent_grads = []
    for m in range(3):
        @pl.loop(0, quarters)
        def _(q, m=m):
            wg_out[m, :, columns(q)] = jnp.dot(
                turned[m, pl.ds(unit, unit), :], acts[m // 2, q], preferred_element_type=f32
            ).astype(bf16)

        lent_grads.append(remote(wg_out.at[m], wg_in.at[m], s_wg, (m,), twin))
        go(lent_grads[m])

    for r in SCATTER_ORDER:
        add_second(0, r)
    for r in SCATTER_ORDER:
        add_first(1, r)

    for copy in route_copies:
        copy.wait_recv()
    route_sum[...] = route[own, :] + route_in[0] + route_in[1] + route_in[2]
    slab = rows // quarters

    def slab_of(q):
        return pl.ds(pl.multiple_of(q * slab, slab), slab)

    slab_copies = []
    for s in range(1, quarters):
        slab_copies.append(remote(route_sum.at[slab_of(quarter(s))], route_z.at[quarters - 1 - s], s_rz, (quarters - 1 - s,), z_dev(s)))
        slab_copies[-1].start()

    for m, out_ref in enumerate((gg_ref, gu_ref, gd_ref)):
        lent_grads[m].wait_recv()

        @pl.loop(0, quarters)
        def _(q, m=m, out_ref=out_ref):
            total = jnp.dot(turned[m, pl.ds(0, unit), :], acts[m // 2, q], preferred_element_type=f32)
            out_ref[0, :, columns(q)] = (total + wg_in[m, :, columns(q)].astype(f32)).astype(bf16)

        add_second(1, SCATTER_ORDER[m])

    add_second(1, SCATTER_ORDER[3])
    finish(0, mixed_ref)
    total = route_sum[slab_of(z), :]
    for r in range(1, quarters):
        slot = route_z.at[r - 1]
        remote(slot, slot, s_rz, (r - 1,), z_dev(r)).wait_recv()
        total = total + route_z[r - 1]
    for copy in slab_copies:
        copy.wait_send()
    names = names_wide[slab_of(z), :]
    lane_slab = lax.broadcasted_iota(jnp.int32, (slab, 128), 1)
    picked = jnp.zeros((slab, 128), f32)
    for k in range(topk):
        match = lane_slab.astype(f32) == names[:, k : k + 1]
        value = jnp.sum(jnp.where(match, total, 0.0), axis=1, keepdims=True)
        picked = jnp.where(lane_slab == k, value, picked)
    route_sum[pl.ds(0, slab), :] = picked
    route_ref[...] = route_sum[...].T[:topk, :slab]
    finish(1, token_ref)
    for copy in started:
        copy.wait_send()


def deliver(*refs):
    count = len(refs) // 2
    for src, dst in zip(refs[:count], refs[count:]):
        dst[...] = src[...]


def dense_device(tokens, route_weight, expert_ids, gate_weight, up_weight, down_weight, grad_output):
    quarters = lax.axis_size("expert")
    rows, feat = tokens.shape
    unit, width = gate_weight.shape[1:]
    topk = expert_ids.shape[1]
    f32, bf16 = jnp.float32, jnp.bfloat16
    vmem = pl.BlockSpec(memory_space=pltpu.VMEM)
    hbm = pl.BlockSpec(memory_space=pl.ANY)
    every, both, half = 4 * rows, 2 * unit, rows // 2
    dma = pltpu.SemaphoreType.DMA
    grads = jax.ShapeDtypeStruct((1, unit, width), bf16)
    results = pl.pallas_call(
        dense_kernel,
        out_shape=(
            jax.ShapeDtypeStruct((rows, feat), bf16),
            jax.ShapeDtypeStruct((rows, feat), bf16),
            jax.ShapeDtypeStruct((topk, rows // quarters), f32),
            grads,
            grads,
            grads,
        ),
        in_specs=[hbm, vmem, vmem, hbm, hbm, hbm, hbm],
        out_specs=(vmem,) * 6,
        scratch_shapes=[
            pltpu.VMEM((2, quarters, every, feat), bf16),
            pltpu.VMEM((2, quarters, every, feat), bf16),
            pltpu.VMEM((3, both, width), bf16),
            pltpu.VMEM((every, 128), f32),
            pltpu.VMEM((rows, 128), f32),
            pltpu.VMEM((every, both), f32),
            pltpu.VMEM((every, both), f32),
            pltpu.VMEM((every, both), f32),
            pltpu.VMEM((every, both), bf16),
            pltpu.VMEM((every, both), bf16),
            pltpu.VMEM((every, both), bf16),
            pltpu.VMEM((3, both, every), bf16),
            pltpu.VMEM((2, 2, quarters, half, feat), bf16),
            pltpu.VMEM((2, 2, quarters, rows, feat), bf16),
            pltpu.VMEM((2, quarters - 1, rows, feat), bf16),
            pltpu.VMEM((2, quarters - 1, rows, feat), bf16),
            pltpu.VMEM((2, rows, feat), f32),
            pltpu.VMEM((every, 128), f32),
            pltpu.VMEM((3, rows, 128), f32),
            pltpu.VMEM((rows, 128), f32),
            pltpu.VMEM((quarters - 1, rows // quarters, 128), f32),
            pltpu.VMEM((3, unit, width), bf16),
            pltpu.VMEM((3, unit, width), bf16),
            dma((2, 2, quarters - 1)),
            dma((2, 2, 2, quarters)),
            dma((2, 2, 2, quarters)),
            dma((2, 3)),
            dma((2, 3)),
            dma((5,)),
            dma((2, 2, 2, quarters)),
            dma((2, 2, 2, quarters)),
            dma((2, 2, quarters - 1)),
            dma((2, 3)),
            dma((2, quarters - 1)),
            dma((2, 3)),
        ],
        compiler_params=pltpu.CompilerParams(
            collective_id=0, has_side_effects=True, vmem_limit_bytes=60 * 2**20
        ),
        cost_estimate=pl.CostEstimate(
            flops=18 * every * both * width, bytes_accessed=12 * unit * width, transcendentals=2 * every * both
        ),
    )(tokens, route_weight.T, expert_ids.T, gate_weight, up_weight, down_weight, grad_output)
    count = len(results)
    mixed, token_part, route_part, *weight_grads = pl.pallas_call(
        deliver,
        out_shape=tuple(jax.ShapeDtypeStruct(v.shape, v.dtype) for v in results),
        in_specs=[vmem] * count,
        out_specs=(vmem,) * count,
        compiler_params=pltpu.CompilerParams(vmem_limit_bytes=60 * 2**20),
    )(*results)
    return (mixed, token_part, route_part.T, *weight_grads)


def on_device(tokens, route_weight, expert_ids, *rest):
    shape = (lax.axis_size("dp"), lax.axis_size("expert"))
    experts = shape[0] // PIECES * shape[1]
    dense = shape == (8, 4) and experts == expert_ids.shape[1]
    body = dense_device if dense else slot_device
    return body(tokens, route_weight, expert_ids, *rest)


def solution(mesh):
    return jax.shard_map(
        on_device,
        mesh=mesh,
        in_specs=(
            P("dp", "expert"),
            P("dp", None),
            P("dp", None),
            P("expert", "dp", None),
            P("expert", "dp", None),
            P("expert", "dp", None),
            P("dp", "expert"),
        ),
        out_specs=(
            P("dp", "expert"),
            P("dp", "expert"),
            P(("dp", "expert"), None),
            P("expert", "dp", None),
            P("expert", "dp", None),
            P("expert", "dp", None),
        ),
        check_vma=False,
    )
```

```python
import jax
import jax.numpy as jnp
from jax import lax
from jax.experimental import pallas as pl
from jax.experimental.pallas import tpu as pltpu
from jax.sharding import PartitionSpec as P

PIECES = 4


def contract_last(left_side, right_side):
    return lax.dot_general(
        left_side, right_side, (((1,), (1,)), ((), ())), preferred_element_type=jnp.float32
    )


def contract_first(left_side, right_side):
    return lax.dot_general(
        left_side, right_side, (((0,), (0,)), ((), ())), preferred_element_type=jnp.float32
    )


def silu_parts(gate_act):
    sigmoid_val = jax.nn.sigmoid(gate_act)
    return (gate_act * sigmoid_val, sigmoid_val * (1.0 + gate_act * (1.0 - sigmoid_val)))


def expert_forward(slot_rows, slot_scale, gate_piece, up_piece, down_piece):
    gate_act = contract_last(slot_rows, gate_piece)
    up_act = contract_last(slot_rows, up_piece)
    active, silu_slope = silu_parts(gate_act)
    hidden = (active * up_act).astype(jnp.bfloat16)
    partial_out = jnp.dot(hidden, down_piece, preferred_element_type=jnp.float32)
    scaled = (slot_scale.astype(jnp.float32)[:, None] * partial_out).astype(jnp.bfloat16)
    return (scaled, gate_act, up_act, hidden)


def slot_device(tokens, route_weight, expert_ids, gate_weight, up_weight, down_weight, grad_output):
    groups = lax.axis_size("expert")
    group_index = lax.axis_index("expert")
    data_size = lax.axis_size("dp")
    exp_local = data_size // PIECES
    tok_local, topk_count = expert_ids.shape
    capacity = min(tok_local, 2 * tok_local * topk_count // (exp_local * groups))
    full_tokens, full_grad = (
        lax.all_gather(tokens, "expert", axis=1, tiled=True),
        lax.all_gather(grad_output, "expert", axis=1, tiled=True),
    )
    feature_width = full_tokens.shape[1]
    gate_piece = gate_weight[0]
    up_piece = up_weight[0]
    down_piece = down_weight[0]
    flat_ids = expert_ids.reshape(-1)
    row_count = flat_ids.shape[0]
    owned_rows = flat_ids // exp_local == group_index
    local_ids = flat_ids % exp_local
    chosen = (
        (local_ids[:, None] == jnp.arange(exp_local, dtype=jnp.int32)[None, :])
        & owned_rows[:, None]
    ).astype(jnp.int32)
    slot_ranks = jnp.sum(chosen * (jnp.cumsum(chosen, axis=0) - 1), axis=1)
    slot_count = exp_local * capacity
    slot_pos = jnp.where(owned_rows, local_ids * capacity + slot_ranks, slot_count)
    row_index = jnp.arange(row_count, dtype=jnp.int32)
    row_of = jnp.zeros((slot_count,), jnp.int32).at[slot_pos].set(row_index, mode="drop")
    slot_live = (
        jnp.zeros((slot_count,), jnp.int32).at[slot_pos].set(jnp.ones_like(row_index), mode="drop")
    )
    token_of = row_of // topk_count
    keep_mask = slot_live.astype(tokens.dtype)[:, None]
    slot_weight = route_weight.reshape(-1)[row_of] * slot_live.astype(route_weight.dtype)

    def spread(values):
        trailing = values.shape[1:]
        grouped = values.reshape((exp_local, 1, capacity) + trailing)
        return jnp.broadcast_to(grouped, (exp_local, PIECES, capacity) + trailing).reshape(
            (data_size, capacity) + trailing
        )

    send_rows = spread(full_tokens[token_of] * keep_mask)
    send_weight = spread(slot_weight)
    send_grads = spread(full_grad[token_of] * keep_mask)
    recv_grads = None
    recv_scale = None
    recv_rows, recv_weight = (
        lax.all_to_all(send_rows, "dp", split_axis=0, concat_axis=0, tiled=True),
        lax.all_to_all(send_weight, "dp", split_axis=0, concat_axis=0, tiled=True),
    )
    scaled, gate_act, up_act, hidden = expert_forward(
        recv_rows.reshape(-1, feature_width),
        recv_weight.reshape(-1),
        gate_piece,
        up_piece,
        down_piece,
    )
    returned = lax.all_to_all(
        scaled.reshape(data_size, capacity, feature_width),
        "dp",
        split_axis=0,
        concat_axis=0,
        tiled=True,
    )
    slot_rows = recv_rows.reshape(-1, feature_width)
    wide_token = spread(token_of).reshape(-1)
    wide_live = spread(slot_live).reshape(-1)
    wide_row = spread(row_of).reshape(-1)
    token_place = (
        (wide_token[None, :] == jnp.arange(tok_local, dtype=jnp.int32)[:, None])
        & (wide_live[None, :] > 0)
    ).astype(jnp.bfloat16)
    mixed_sum = jnp.dot(
        token_place, returned.reshape(-1, feature_width), preferred_element_type=jnp.float32
    )
    recv_grads, recv_scale = (
        lax.all_to_all(send_grads, "dp", split_axis=0, concat_axis=0, tiled=True),
        lax.all_to_all(send_weight, "dp", split_axis=0, concat_axis=0, tiled=True),
    )
    active, silu_slope = silu_parts(gate_act)
    slot_grads = recv_grads.reshape(-1, feature_width)
    weight_wide = recv_scale.reshape(-1).astype(jnp.float32)[:, None]
    into_hidden = contract_last(slot_grads, down_piece)
    route_terms = jnp.sum(into_hidden * hidden.astype(jnp.float32), axis=1).astype(jnp.bfloat16)
    hidden_grad = weight_wide * into_hidden
    gate_grad = (hidden_grad * up_act * silu_slope).astype(jnp.bfloat16)
    up_grad = (hidden_grad * active).astype(jnp.bfloat16)
    row_grad = (
        jnp.dot(gate_grad, gate_piece, preferred_element_type=jnp.float32)
        + jnp.dot(up_grad, up_piece, preferred_element_type=jnp.float32)
    ).astype(jnp.bfloat16)
    scaled_grad = (weight_wide * slot_grads.astype(jnp.float32)).astype(jnp.bfloat16)
    grad_gate = contract_first(gate_grad, slot_rows).astype(jnp.bfloat16)[None]
    grad_up = contract_first(up_grad, slot_rows).astype(jnp.bfloat16)[None]
    grad_down = contract_first(hidden, scaled_grad).astype(jnp.bfloat16)[None]
    back_rows, back_terms = (
        lax.all_to_all(
            row_grad.reshape(data_size, capacity, feature_width),
            "dp",
            split_axis=0,
            concat_axis=0,
            tiled=True,
        ),
        lax.all_to_all(
            route_terms.reshape(data_size, capacity), "dp", split_axis=0, concat_axis=0, tiled=True
        ),
    )
    token_sum = jnp.dot(
        token_place, back_rows.reshape(-1, feature_width), preferred_element_type=jnp.float32
    )
    row_place = (
        (wide_row[None, :] == jnp.arange(row_count, dtype=jnp.int32)[:, None])
        & (wide_live[None, :] > 0)
    ).astype(jnp.bfloat16)
    route_sum = jnp.dot(
        row_place, back_terms.reshape(-1), preferred_element_type=jnp.float32
    ).reshape(tok_local, topk_count)
    mixed_part, token_part, route_part = (
        lax.psum_scatter(mixed_sum, "expert", scatter_dimension=1, tiled=True),
        lax.psum_scatter(token_sum, "expert", scatter_dimension=1, tiled=True),
        lax.psum_scatter(route_sum, "expert", scatter_dimension=0, tiled=True),
    )
    return (
        mixed_part.astype(jnp.bfloat16),
        token_part.astype(jnp.bfloat16),
        route_part,
        grad_gate,
        grad_up,
        grad_down,
    )


MESH = pl.DeviceIdType.MESH
GATHER_ORDER = (0, 1, 3, 2)
SCATTER_ORDER = (2, 1, 3, 0)


def remote(src, dst, sems, index, device):
    return pltpu.make_async_remote_copy(
        src_ref=src,
        dst_ref=dst,
        send_sem=sems.at[(0,) + index],
        recv_sem=sems.at[(1,) + index],
        device_id=device,
        device_id_type=MESH,
    )


def dense_kernel(
    tok_ref, rw_ref, ids_ref, wg_ref, wu_ref, wd_ref, gy_ref,
    mixed_ref, token_ref, route_ref, gg_ref, gu_ref, gd_ref,
    acts, parts, weights, wide, names_wide, gate, up, into, hw, gg, ug, turned,
    half_in, full_in, z_out, z_in, z_own, route, route_in, route_sum, route_z, wg_out, wg_in,
    s_z, s_plane, s_fwd, s_wide, s_wt, s_local, s_r1, s_r2, s_r3, s_rt, s_rz, s_wg,
):
    f32, bf16 = jnp.float32, jnp.bfloat16
    rows, feat = tok_ref.shape
    unit = wg_ref.shape[1]
    topk = ids_ref.shape[0]
    half = rows // 2
    quarters = acts.shape[1]
    d, z = lax.axis_index("dp"), lax.axis_index("expert")
    core, x, y = lax.rem(d, 2), lax.rem(d // 2, 2), d // 4
    x_dev = (y * 4 + (1 - x) * 2 + core, z)
    y_dev = ((1 - y) * 4 + x * 2 + core, z)
    diag_dev = ((1 - y) * 4 + (1 - x) * 2 + core, z)
    twin = (y * 4 + x * 2 + (1 - core), z)
    expert = z * (lax.axis_size("dp") // PIECES) + d // PIECES

    def quarter(r):
        return lax.rem(z + r, quarters)

    def z_dev(r):
        return (d, quarter(r))

    barrier = pltpu.get_barrier_semaphore()
    others = [x_dev, y_dev, diag_dev, twin] + [z_dev(r) for r in range(1, quarters)]
    for dev in others:
        pl.semaphore_signal(barrier, inc=1, device_id=dev, device_id_type=MESH)
    pl.semaphore_wait(barrier, len(others))

    own, at_x, at_y, at_d = (pl.ds(i * rows, rows) for i in range(4))
    d_top, d_low = pl.ds(3 * rows, half), pl.ds(3 * rows + half, half)
    x_top, x_low = pl.ds(rows, half), pl.ds(rows + half, half)
    y_top, y_low = pl.ds(2 * rows, half), pl.ds(2 * rows + half, half)
    started = []

    def go(copy):
        copy.start()
        started.append(copy)

    def z_send(a, s):
        return remote((tok_ref, gy_ref)[a], acts.at[a, z, own], s_z, (a, quarters - 1 - s), z_dev(s))

    def z_arrive(a, r):
        block = acts.at[a, quarter(r), own]
        remote(block, block, s_z, (a, r - 1), z_dev(r)).wait_recv()

    def plane(a, r):
        q = quarter(r)
        src = (tok_ref, gy_ref)[a] if r == 0 else acts.at[a, q, own]
        return (
            remote(src, acts.at[a, q, at_x], s_plane, (a, 0, r), x_dev),
            remote(src, acts.at[a, q, at_y], s_plane, (a, 1, r), y_dev),
        )

    def forward(a, r):
        q = quarter(r)
        return (
            remote(acts.at[a, q, x_top], acts.at[a, q, d_top], s_fwd, (a, 0, r), y_dev),
            remote(acts.at[a, q, y_low], acts.at[a, q, d_low], s_fwd, (a, 1, r), x_dev),
        )

    def send_plane(a, r):
        for copy in plane(a, r):
            go(copy)

    def pass_on(a, r):
        for arrived, onward in zip(plane(a, r), forward(a, r)):
            arrived.wait_recv()
            go(onward)

    def complete(a, r):
        for copy in forward(a, r):
            copy.wait_recv()

    for s in (1, 3, 2):
        go(z_send(0, s))
    send_plane(0, 0)
    send_plane(1, 0)
    local, lent = [], []
    for a, ref in enumerate((tok_ref, gy_ref)):
        local.append(pltpu.make_async_copy(ref, acts.at[a, z, own], s_local.at[3 + a]))
        local[a].start()
    for m, ref in enumerate((wg_ref, wu_ref, wd_ref)):
        copy = pltpu.make_async_copy(ref.at[0], weights.at[m, pl.ds(0, unit)], s_local.at[m])
        copy.start()
        local.append(copy)
        lent.append(remote(ref.at[0], weights.at[m, pl.ds(unit, unit)], s_wt, (m,), twin))
        go(lent[m])

    lane = lax.broadcasted_iota(jnp.int32, (rows, 128), 1)
    ids, rw = ids_ref[...], rw_ref[...].astype(f32)
    level = lax.broadcasted_iota(jnp.int32, (128, rows), 0)
    spread, named = jnp.zeros((128, rows), f32), jnp.zeros((128, rows), f32)
    for k in range(topk):
        spread = spread + jnp.where(level == ids[k : k + 1, :], rw[k : k + 1, :], 0.0)
        named = named + jnp.where(level == k, ids[k : k + 1, :].astype(f32), 0.0)
    wide[own, :] = spread.T
    names_wide[...] = named.T
    wide_copies = [
        remote(wide.at[own], wide.at[place], s_wide, (i,), dev)
        for i, (place, dev) in enumerate(((at_x, x_dev), (at_y, y_dev), (at_d, diag_dev)))
    ]
    for copy in wide_copies:
        go(copy)
    for i, r in enumerate(GATHER_ORDER[1:]):
        z_arrive(0, r)
        send_plane(0, r)
        if i < 2:
            pass_on(i, 0)
    for s in (1, 3, 2):
        go(z_send(1, s))
    for copy in local:
        copy.wait()
    for copy in lent:
        copy.wait_recv()

    def columns(q):
        return pl.ds(pl.multiple_of(q * feat, feat), feat)

    def add_forward(i, r):
        q = quarter(r)
        for total, m in ((gate, 0), (up, 1)):
            term = contract_last(acts[0, q], weights[m, :, columns(q)])
            total[...] = term if i == 0 else total[...] + term

    for i, r in enumerate(GATHER_ORDER):
        if i > 0:
            pass_on(0, r)
            z_arrive(1, r)
            send_plane(1, r)
            complete(0, GATHER_ORDER[i - 1])
            add_forward(i - 1, GATHER_ORDER[i - 1])
    complete(0, GATHER_ORDER[-1])
    add_forward(len(GATHER_ORDER) - 1, GATHER_ORDER[-1])
    for copy in wide_copies:
        copy.wait_recv()

    def block_rows(b):
        return pl.ds(pl.multiple_of(b * rows, rows), rows)

    def scale_of(b):
        return jnp.sum(jnp.where(lane == expert, wide[block_rows(b), :], 0.0), axis=1, keepdims=True)

    @pl.loop(0, 4)
    def _(b):
        at = block_rows(b)
        active, _slope = silu_parts(gate[at, :])
        weighted = scale_of(b) * (active * up[at, :])
        hw[at, :] = weighted.astype(bf16)
        turned[2, :, at] = weighted.T.astype(bf16)

    def first(a, r):
        q = quarter(r)
        return (
            remote(parts.at[a, q, d_top], half_in.at[a, 0, r], s_r1, (a, 0, r), x_dev),
            remote(parts.at[a, q, d_low], half_in.at[a, 1, r], s_r1, (a, 1, r), y_dev),
        )

    def second(a, r):
        q = quarter(r)
        return (
            remote(parts.at[a, q, at_x], full_in.at[a, 0, r], s_r2, (a, 0, r), x_dev),
            remote(parts.at[a, q, at_y], full_in.at[a, 1, r], s_r2, (a, 1, r), y_dev),
        )

    def send_first(a, r):
        for copy in first(a, r):
            go(copy)

    def add_first(a, r):
        q = quarter(r)
        for i, (copy, place) in enumerate(zip(first(a, r), (y_top, x_low))):
            copy.wait_recv()
            here = parts[a, q, place, :].astype(f32) + half_in[a, i, r].astype(f32)
            parts[a, q, place, :] = here.astype(bf16)
        for copy in second(a, r):
            go(copy)

    def third(a, r):
        return remote(z_out.at[a, r - 1], z_in.at[a, quarters - 1 - r], s_r3, (a, quarters - 1 - r), z_dev(r))

    def add_second(a, r):
        for copy in second(a, r):
            copy.wait_recv()
        total = parts[a, quarter(r), own, :].astype(f32)
        total = total + full_in[a, 0, r].astype(f32) + full_in[a, 1, r].astype(f32)
        if r == 0:
            z_own[a] = total
        else:
            z_out[a, r - 1] = total.astype(bf16)
            go(third(a, r))

    def finish(a, out_ref):
        total = z_own[a]
        for r in range(1, quarters):
            slot = z_in.at[a, r - 1]
            remote(slot, slot, s_r3, (a, r - 1), z_dev(r)).wait_recv()
            total = total + z_in[a, r - 1].astype(f32)
        out_ref[...] = total.astype(bf16)

    for near, r in zip(GATHER_ORDER, SCATTER_ORDER):
        q = quarter(r)
        if near > 0:
            pass_on(1, near)
        parts[0, q] = jnp.dot(
            hw[...], weights[2, :, columns(q)], preferred_element_type=f32
        ).astype(bf16)
        send_first(0, r)

    for i, (near, r) in enumerate(zip(GATHER_ORDER, SCATTER_ORDER)):
        q = quarter(near)
        complete(1, near)
        term = contract_last(acts[1, q], weights[2, :, columns(q)])
        into[...] = term if i == 0 else into[...] + term
        add_first(0, r)

    @pl.loop(0, 4)
    def _(b):
        at = block_rows(b)
        gate_act, up_act, back = gate[at, :], up[at, :], into[at, :]
        active, slope = silu_parts(gate_act)
        term = jnp.sum(back * (active * up_act), axis=1, keepdims=True)
        route[at, :] = jnp.where(lane == expert, term, 0.0)
        scaled = scale_of(b) * back
        gate_grad, up_grad = scaled * up_act * slope, scaled * active
        gg[at, :] = gate_grad.astype(bf16)
        ug[at, :] = up_grad.astype(bf16)
        turned[0, :, at] = gate_grad.T.astype(bf16)
        turned[1, :, at] = up_grad.T.astype(bf16)

    for r in SCATTER_ORDER:
        q = quarter(r)
        total = jnp.dot(gg[...], weights[0, :, columns(q)], preferred_element_type=f32)
        total = total + jnp.dot(ug[...], weights[1, :, columns(q)], preferred_element_type=f32)
        parts[1, q] = total.astype(bf16)
        send_first(1, r)
    route_copies = [
        remote(route.at[place], route_in.at[i], s_rt, (i,), dev)
        for i, (place, dev) in enumerate(((at_x, x_dev), (at_y, y_dev), (at_d, diag_dev)))
    ]
    for copy in route_copies:
        go(copy)

    lent_grads = []
    for m in range(3):
        @pl.loop(0, quarters)
        def _(q, m=m):
            wg_out[m, :, columns(q)] = jnp.dot(
                turned[m, pl.ds(unit, unit), :], acts[m // 2, q], preferred_element_type=f32
            ).astype(bf16)

        lent_grads.append(remote(wg_out.at[m], wg_in.at[m], s_wg, (m,), twin))
        go(lent_grads[m])

    for r in SCATTER_ORDER:
        add_second(0, r)
    for r in SCATTER_ORDER[:2]:
        add_first(1, r)

    for copy in route_copies:
        copy.wait_recv()
    route_sum[...] = route[own, :] + route_in[0] + route_in[1] + route_in[2]
    slab = rows // quarters

    def slab_of(q):
        return pl.ds(pl.multiple_of(q * slab, slab), slab)

    slab_copies = []
    for s in range(1, quarters):
        slab_copies.append(remote(route_sum.at[slab_of(quarter(s))], route_z.at[quarters - 1 - s], s_rz, (quarters - 1 - s,), z_dev(s)))
        slab_copies[-1].start()

    for m, out_ref in enumerate((gg_ref, gu_ref, gd_ref)):
        lent_grads[m].wait_recv()

        @pl.loop(0, quarters)
        def _(q, m=m, out_ref=out_ref):
            total = jnp.dot(turned[m, pl.ds(0, unit), :], acts[m // 2, q], preferred_element_type=f32)
            out_ref[0, :, columns(q)] = (total + wg_in[m, :, columns(q)].astype(f32)).astype(bf16)

        if m < 2:
            add_first(1, SCATTER_ORDER[m + 2])
        add_second(1, SCATTER_ORDER[m])

    add_second(1, SCATTER_ORDER[3])
    finish(0, mixed_ref)
    total = route_sum[slab_of(z), :]
    for r in range(1, quarters):
        slot = route_z.at[r - 1]
        remote(slot, slot, s_rz, (r - 1,), z_dev(r)).wait_recv()
        total = total + route_z[r - 1]
    for copy in slab_copies:
        copy.wait_send()
    names = names_wide[slab_of(z), :]
    lane_slab = lax.broadcasted_iota(jnp.int32, (slab, 128), 1)
    picked = jnp.zeros((slab, 128), f32)
    for k in range(topk):
        match = lane_slab.astype(f32) == names[:, k : k + 1]
        value = jnp.sum(jnp.where(match, total, 0.0), axis=1, keepdims=True)
        picked = jnp.where(lane_slab == k, value, picked)
    route_sum[pl.ds(0, slab), :] = picked
    route_ref[...] = route_sum[...].T[:topk, :slab]
    finish(1, token_ref)
    for copy in started:
        copy.wait_send()


def deliver(*refs):
    count = len(refs) // 2
    for src, dst in zip(refs[:count], refs[count:]):
        dst[...] = src[...]


def dense_device(tokens, route_weight, expert_ids, gate_weight, up_weight, down_weight, grad_output):
    quarters = lax.axis_size("expert")
    rows, feat = tokens.shape
    unit, width = gate_weight.shape[1:]
    topk = expert_ids.shape[1]
    f32, bf16 = jnp.float32, jnp.bfloat16
    vmem = pl.BlockSpec(memory_space=pltpu.VMEM)
    hbm = pl.BlockSpec(memory_space=pl.ANY)
    every, both, half = 4 * rows, 2 * unit, rows // 2
    dma = pltpu.SemaphoreType.DMA
    grads = jax.ShapeDtypeStruct((1, unit, width), bf16)
    results = pl.pallas_call(
        dense_kernel,
        out_shape=(
            jax.ShapeDtypeStruct((rows, feat), bf16),
            jax.ShapeDtypeStruct((rows, feat), bf16),
            jax.ShapeDtypeStruct((topk, rows // quarters), f32),
            grads,
            grads,
            grads,
        ),
        in_specs=[hbm, vmem, vmem, hbm, hbm, hbm, hbm],
        out_specs=(vmem,) * 6,
        scratch_shapes=[
            pltpu.VMEM((2, quarters, every, feat), bf16),
            pltpu.VMEM((2, quarters, every, feat), bf16),
            pltpu.VMEM((3, both, width), bf16),
            pltpu.VMEM((every, 128), f32),
            pltpu.VMEM((rows, 128), f32),
            pltpu.VMEM((every, both), f32),
            pltpu.VMEM((every, both), f32),
            pltpu.VMEM((every, both), f32),
            pltpu.VMEM((every, both), bf16),
            pltpu.VMEM((every, both), bf16),
            pltpu.VMEM((every, both), bf16),
            pltpu.VMEM((3, both, every), bf16),
            pltpu.VMEM((2, 2, quarters, half, feat), bf16),
            pltpu.VMEM((2, 2, quarters, rows, feat), bf16),
            pltpu.VMEM((2, quarters - 1, rows, feat), bf16),
            pltpu.VMEM((2, quarters - 1, rows, feat), bf16),
            pltpu.VMEM((2, rows, feat), f32),
            pltpu.VMEM((every, 128), f32),
            pltpu.VMEM((3, rows, 128), f32),
            pltpu.VMEM((rows, 128), f32),
            pltpu.VMEM((quarters - 1, rows // quarters, 128), f32),
            pltpu.VMEM((3, unit, width), bf16),
            pltpu.VMEM((3, unit, width), bf16),
            dma((2, 2, quarters - 1)),
            dma((2, 2, 2, quarters)),
            dma((2, 2, 2, quarters)),
            dma((2, 3)),
            dma((2, 3)),
            dma((5,)),
            dma((2, 2, 2, quarters)),
            dma((2, 2, 2, quarters)),
            dma((2, 2, quarters - 1)),
            dma((2, 3)),
            dma((2, quarters - 1)),
            dma((2, 3)),
        ],
        compiler_params=pltpu.CompilerParams(
            collective_id=0, has_side_effects=True, vmem_limit_bytes=60 * 2**20
        ),
        cost_estimate=pl.CostEstimate(
            flops=18 * every * both * width, bytes_accessed=12 * unit * width, transcendentals=2 * every * both
        ),
    )(tokens, route_weight.T, expert_ids.T, gate_weight, up_weight, down_weight, grad_output)
    count = len(results)
    mixed, token_part, route_part, *weight_grads = pl.pallas_call(
        deliver,
        out_shape=tuple(jax.ShapeDtypeStruct(v.shape, v.dtype) for v in results),
        in_specs=[vmem] * count,
        out_specs=(vmem,) * count,
        compiler_params=pltpu.CompilerParams(vmem_limit_bytes=60 * 2**20),
    )(*results)
    return (mixed, token_part, route_part.T, *weight_grads)


def on_device(tokens, route_weight, expert_ids, *rest):
    shape = (lax.axis_size("dp"), lax.axis_size("expert"))
    experts = shape[0] // PIECES * shape[1]
    dense = shape == (8, 4) and experts == expert_ids.shape[1]
    body = dense_device if dense else slot_device
    return body(tokens, route_weight, expert_ids, *rest)


def solution(mesh):
    return jax.shard_map(
        on_device,
        mesh=mesh,
        in_specs=(
            P("dp", "expert"),
            P("dp", None),
            P("dp", None),
            P("expert", "dp", None),
            P("expert", "dp", None),
            P("expert", "dp", None),
            P("dp", "expert"),
        ),
        out_specs=(
            P("dp", "expert"),
            P("dp", "expert"),
            P(("dp", "expert"), None),
            P("expert", "dp", None),
            P("expert", "dp", None),
            P("expert", "dp", None),
        ),
        check_vma=False,
    )
```

```python
import jax
import jax.numpy as jnp
from jax import lax
from jax.experimental import pallas as pl
from jax.experimental.pallas import tpu as pltpu
from jax.sharding import PartitionSpec as P

PIECES = 4


def contract_last(left_side, right_side):
    return lax.dot_general(
        left_side, right_side, (((1,), (1,)), ((), ())), preferred_element_type=jnp.float32
    )


def contract_first(left_side, right_side):
    return lax.dot_general(
        left_side, right_side, (((0,), (0,)), ((), ())), preferred_element_type=jnp.float32
    )


def silu_parts(gate_act):
    sigmoid_val = jax.nn.sigmoid(gate_act)
    return (gate_act * sigmoid_val, sigmoid_val * (1.0 + gate_act * (1.0 - sigmoid_val)))


def expert_forward(slot_rows, slot_scale, gate_piece, up_piece, down_piece):
    gate_act = contract_last(slot_rows, gate_piece)
    up_act = contract_last(slot_rows, up_piece)
    active, silu_slope = silu_parts(gate_act)
    hidden = (active * up_act).astype(jnp.bfloat16)
    partial_out = jnp.dot(hidden, down_piece, preferred_element_type=jnp.float32)
    scaled = (slot_scale.astype(jnp.float32)[:, None] * partial_out).astype(jnp.bfloat16)
    return (scaled, gate_act, up_act, hidden)


def slot_device(tokens, route_weight, expert_ids, gate_weight, up_weight, down_weight, grad_output):
    groups = lax.axis_size("expert")
    group_index = lax.axis_index("expert")
    data_size = lax.axis_size("dp")
    exp_local = data_size // PIECES
    tok_local, topk_count = expert_ids.shape
    capacity = min(tok_local, 2 * tok_local * topk_count // (exp_local * groups))
    full_tokens, full_grad = (
        lax.all_gather(tokens, "expert", axis=1, tiled=True),
        lax.all_gather(grad_output, "expert", axis=1, tiled=True),
    )
    feature_width = full_tokens.shape[1]
    gate_piece = gate_weight[0]
    up_piece = up_weight[0]
    down_piece = down_weight[0]
    flat_ids = expert_ids.reshape(-1)
    row_count = flat_ids.shape[0]
    owned_rows = flat_ids // exp_local == group_index
    local_ids = flat_ids % exp_local
    chosen = (
        (local_ids[:, None] == jnp.arange(exp_local, dtype=jnp.int32)[None, :])
        & owned_rows[:, None]
    ).astype(jnp.int32)
    slot_ranks = jnp.sum(chosen * (jnp.cumsum(chosen, axis=0) - 1), axis=1)
    slot_count = exp_local * capacity
    slot_pos = jnp.where(owned_rows, local_ids * capacity + slot_ranks, slot_count)
    row_index = jnp.arange(row_count, dtype=jnp.int32)
    row_of = jnp.zeros((slot_count,), jnp.int32).at[slot_pos].set(row_index, mode="drop")
    slot_live = (
        jnp.zeros((slot_count,), jnp.int32).at[slot_pos].set(jnp.ones_like(row_index), mode="drop")
    )
    token_of = row_of // topk_count
    keep_mask = slot_live.astype(tokens.dtype)[:, None]
    slot_weight = route_weight.reshape(-1)[row_of] * slot_live.astype(route_weight.dtype)

    def spread(values):
        trailing = values.shape[1:]
        grouped = values.reshape((exp_local, 1, capacity) + trailing)
        return jnp.broadcast_to(grouped, (exp_local, PIECES, capacity) + trailing).reshape(
            (data_size, capacity) + trailing
        )

    send_rows = spread(full_tokens[token_of] * keep_mask)
    send_weight = spread(slot_weight)
    send_grads = spread(full_grad[token_of] * keep_mask)
    recv_grads = None
    recv_scale = None
    recv_rows, recv_weight = (
        lax.all_to_all(send_rows, "dp", split_axis=0, concat_axis=0, tiled=True),
        lax.all_to_all(send_weight, "dp", split_axis=0, concat_axis=0, tiled=True),
    )
    scaled, gate_act, up_act, hidden = expert_forward(
        recv_rows.reshape(-1, feature_width),
        recv_weight.reshape(-1),
        gate_piece,
        up_piece,
        down_piece,
    )
    returned = lax.all_to_all(
        scaled.reshape(data_size, capacity, feature_width),
        "dp",
        split_axis=0,
        concat_axis=0,
        tiled=True,
    )
    slot_rows = recv_rows.reshape(-1, feature_width)
    wide_token = spread(token_of).reshape(-1)
    wide_live = spread(slot_live).reshape(-1)
    wide_row = spread(row_of).reshape(-1)
    token_place = (
        (wide_token[None, :] == jnp.arange(tok_local, dtype=jnp.int32)[:, None])
        & (wide_live[None, :] > 0)
    ).astype(jnp.bfloat16)
    mixed_sum = jnp.dot(
        token_place, returned.reshape(-1, feature_width), preferred_element_type=jnp.float32
    )
    recv_grads, recv_scale = (
        lax.all_to_all(send_grads, "dp", split_axis=0, concat_axis=0, tiled=True),
        lax.all_to_all(send_weight, "dp", split_axis=0, concat_axis=0, tiled=True),
    )
    active, silu_slope = silu_parts(gate_act)
    slot_grads = recv_grads.reshape(-1, feature_width)
    weight_wide = recv_scale.reshape(-1).astype(jnp.float32)[:, None]
    into_hidden = contract_last(slot_grads, down_piece)
    route_terms = jnp.sum(into_hidden * hidden.astype(jnp.float32), axis=1).astype(jnp.bfloat16)
    hidden_grad = weight_wide * into_hidden
    gate_grad = (hidden_grad * up_act * silu_slope).astype(jnp.bfloat16)
    up_grad = (hidden_grad * active).astype(jnp.bfloat16)
    row_grad = (
        jnp.dot(gate_grad, gate_piece, preferred_element_type=jnp.float32)
        + jnp.dot(up_grad, up_piece, preferred_element_type=jnp.float32)
    ).astype(jnp.bfloat16)
    scaled_grad = (weight_wide * slot_grads.astype(jnp.float32)).astype(jnp.bfloat16)
    grad_gate = contract_first(gate_grad, slot_rows).astype(jnp.bfloat16)[None]
    grad_up = contract_first(up_grad, slot_rows).astype(jnp.bfloat16)[None]
    grad_down = contract_first(hidden, scaled_grad).astype(jnp.bfloat16)[None]
    back_rows, back_terms = (
        lax.all_to_all(
            row_grad.reshape(data_size, capacity, feature_width),
            "dp",
            split_axis=0,
            concat_axis=0,
            tiled=True,
        ),
        lax.all_to_all(
            route_terms.reshape(data_size, capacity), "dp", split_axis=0, concat_axis=0, tiled=True
        ),
    )
    token_sum = jnp.dot(
        token_place, back_rows.reshape(-1, feature_width), preferred_element_type=jnp.float32
    )
    row_place = (
        (wide_row[None, :] == jnp.arange(row_count, dtype=jnp.int32)[:, None])
        & (wide_live[None, :] > 0)
    ).astype(jnp.bfloat16)
    route_sum = jnp.dot(
        row_place, back_terms.reshape(-1), preferred_element_type=jnp.float32
    ).reshape(tok_local, topk_count)
    mixed_part, token_part, route_part = (
        lax.psum_scatter(mixed_sum, "expert", scatter_dimension=1, tiled=True),
        lax.psum_scatter(token_sum, "expert", scatter_dimension=1, tiled=True),
        lax.psum_scatter(route_sum, "expert", scatter_dimension=0, tiled=True),
    )
    return (
        mixed_part.astype(jnp.bfloat16),
        token_part.astype(jnp.bfloat16),
        route_part,
        grad_gate,
        grad_up,
        grad_down,
    )


MESH = pl.DeviceIdType.MESH
GATHER_ORDER = (0, 1, 3, 2)
SCATTER_ORDER = (2, 1, 3, 0)


def remote(src, dst, sems, index, device):
    return pltpu.make_async_remote_copy(
        src_ref=src,
        dst_ref=dst,
        send_sem=sems.at[(0,) + index],
        recv_sem=sems.at[(1,) + index],
        device_id=device,
        device_id_type=MESH,
    )


def dense_kernel(
    tok_ref, rw_ref, ids_ref, wg_ref, wu_ref, wd_ref, gy_ref,
    mixed_ref, token_ref, route_ref, gg_ref, gu_ref, gd_ref,
    acts, parts, weights, wide, names_wide, gate, up, into, hw, gg, ug, turned,
    half_in, full_in, z_out, z_in, z_own, route, route_in, route_sum, route_z, wg_out, wg_in,
    s_z, s_plane, s_fwd, s_wide, s_wt, s_local, s_r1, s_r2, s_r3, s_rt, s_rz, s_wg,
):
    f32, bf16 = jnp.float32, jnp.bfloat16
    rows, feat = tok_ref.shape
    unit = wg_ref.shape[1]
    topk = ids_ref.shape[0]
    half = rows // 2
    quarters = acts.shape[1]
    d, z = lax.axis_index("dp"), lax.axis_index("expert")
    core, x, y = lax.rem(d, 2), lax.rem(d // 2, 2), d // 4
    x_dev = (y * 4 + (1 - x) * 2 + core, z)
    y_dev = ((1 - y) * 4 + x * 2 + core, z)
    diag_dev = ((1 - y) * 4 + (1 - x) * 2 + core, z)
    twin = (y * 4 + x * 2 + (1 - core), z)
    expert = z * (lax.axis_size("dp") // PIECES) + d // PIECES

    def quarter(r):
        return lax.rem(z + r, quarters)

    def z_dev(r):
        return (d, quarter(r))

    barrier = pltpu.get_barrier_semaphore()
    others = [x_dev, y_dev, diag_dev, twin] + [z_dev(r) for r in range(1, quarters)]
    for dev in others:
        pl.semaphore_signal(barrier, inc=1, device_id=dev, device_id_type=MESH)
    pl.semaphore_wait(barrier, len(others))

    own, at_x, at_y, at_d = (pl.ds(i * rows, rows) for i in range(4))
    d_top, d_low = pl.ds(3 * rows, half), pl.ds(3 * rows + half, half)
    x_top, x_low = pl.ds(rows, half), pl.ds(rows + half, half)
    y_top, y_low = pl.ds(2 * rows, half), pl.ds(2 * rows + half, half)
    started = []

    def go(copy):
        copy.start()
        started.append(copy)

    def z_send(a, s):
        return remote((tok_ref, gy_ref)[a], acts.at[a, z, own], s_z, (a, quarters - 1 - s), z_dev(s))

    def z_arrive(a, r):
        block = acts.at[a, quarter(r), own]
        remote(block, block, s_z, (a, r - 1), z_dev(r)).wait_recv()

    def plane(a, r):
        q = quarter(r)
        src = (tok_ref, gy_ref)[a] if r == 0 else acts.at[a, q, own]
        return (
            remote(src, acts.at[a, q, at_x], s_plane, (a, 0, r), x_dev),
            remote(src, acts.at[a, q, at_y], s_plane, (a, 1, r), y_dev),
        )

    def forward(a, r):
        q = quarter(r)
        return (
            remote(acts.at[a, q, x_top], acts.at[a, q, d_top], s_fwd, (a, 0, r), y_dev),
            remote(acts.at[a, q, y_low], acts.at[a, q, d_low], s_fwd, (a, 1, r), x_dev),
        )

    def send_plane(a, r):
        for copy in plane(a, r):
            go(copy)

    def pass_on(a, r):
        for arrived, onward in zip(plane(a, r), forward(a, r)):
            arrived.wait_recv()
            go(onward)

    def complete(a, r):
        for copy in forward(a, r):
            copy.wait_recv()

    for s in (1, 3, 2):
        go(z_send(0, s))
    send_plane(0, 0)
    send_plane(1, 0)
    local, lent = [], []
    for a, ref in enumerate((tok_ref, gy_ref)):
        local.append(pltpu.make_async_copy(ref, acts.at[a, z, own], s_local.at[3 + a]))
        local[a].start()
    for m, ref in enumerate((wg_ref, wu_ref, wd_ref)):
        copy = pltpu.make_async_copy(ref.at[0], weights.at[m, pl.ds(0, unit)], s_local.at[m])
        copy.start()
        local.append(copy)
        lent.append(remote(ref.at[0], weights.at[m, pl.ds(unit, unit)], s_wt, (m,), twin))
        go(lent[m])

    lane = lax.broadcasted_iota(jnp.int32, (rows, 128), 1)
    ids, rw = ids_ref[...], rw_ref[...].astype(f32)
    level = lax.broadcasted_iota(jnp.int32, (128, rows), 0)
    spread, named = jnp.zeros((128, rows), f32), jnp.zeros((128, rows), f32)
    for k in range(topk):
        spread = spread + jnp.where(level == ids[k : k + 1, :], rw[k : k + 1, :], 0.0)
        named = named + jnp.where(level == k, ids[k : k + 1, :].astype(f32), 0.0)
    wide[own, :] = spread.T
    names_wide[...] = named.T
    wide_copies = [
        remote(wide.at[own], wide.at[place], s_wide, (i,), dev)
        for i, (place, dev) in enumerate(((at_x, x_dev), (at_y, y_dev), (at_d, diag_dev)))
    ]
    for copy in wide_copies:
        go(copy)
    for i, r in enumerate(GATHER_ORDER[1:]):
        z_arrive(0, r)
        send_plane(0, r)
        if i < 2:
            pass_on(i, 0)
        if i == 1:
            for s in (1, 3, 2):
                go(z_send(1, s))
    for copy in local:
        copy.wait()
    for copy in lent:
        copy.wait_recv()

    def columns(q):
        return pl.ds(pl.multiple_of(q * feat, feat), feat)

    def add_forward(i, r):
        q = quarter(r)
        for total, m in ((gate, 0), (up, 1)):
            term = contract_last(acts[0, q], weights[m, :, columns(q)])
            total[...] = term if i == 0 else total[...] + term

    for i, r in enumerate(GATHER_ORDER):
        if i > 0:
            pass_on(0, r)
            complete(0, GATHER_ORDER[i - 1])
            add_forward(i - 1, GATHER_ORDER[i - 1])
    for r in GATHER_ORDER[1:]:
        z_arrive(1, r)
        send_plane(1, r)
    complete(0, GATHER_ORDER[-1])
    add_forward(len(GATHER_ORDER) - 1, GATHER_ORDER[-1])
    for copy in wide_copies:
        copy.wait_recv()

    def block_rows(b):
        return pl.ds(pl.multiple_of(b * rows, rows), rows)

    def scale_of(b):
        return jnp.sum(jnp.where(lane == expert, wide[block_rows(b), :], 0.0), axis=1, keepdims=True)

    @pl.loop(0, 4)
    def _(b):
        at = block_rows(b)
        active, _slope = silu_parts(gate[at, :])
        weighted = scale_of(b) * (active * up[at, :])
        hw[at, :] = weighted.astype(bf16)
        turned[2, :, at] = weighted.T.astype(bf16)

    def first(a, r):
        q = quarter(r)
        return (
            remote(parts.at[a, q, d_top], half_in.at[a, 0, r], s_r1, (a, 0, r), x_dev),
            remote(parts.at[a, q, d_low], half_in.at[a, 1, r], s_r1, (a, 1, r), y_dev),
        )

    def second(a, r):
        q = quarter(r)
        return (
            remote(parts.at[a, q, at_x], full_in.at[a, 0, r], s_r2, (a, 0, r), x_dev),
            remote(parts.at[a, q, at_y], full_in.at[a, 1, r], s_r2, (a, 1, r), y_dev),
        )

    def send_first(a, r):
        for copy in first(a, r):
            go(copy)

    def add_first(a, r):
        q = quarter(r)
        for i, (copy, place) in enumerate(zip(first(a, r), (y_top, x_low))):
            copy.wait_recv()
            here = parts[a, q, place, :].astype(f32) + half_in[a, i, r].astype(f32)
            parts[a, q, place, :] = here.astype(bf16)
        for copy in second(a, r):
            go(copy)

    def third(a, r):
        return remote(z_out.at[a, r - 1], z_in.at[a, quarters - 1 - r], s_r3, (a, quarters - 1 - r), z_dev(r))

    def add_second(a, r):
        for copy in second(a, r):
            copy.wait_recv()
        total = parts[a, quarter(r), own, :].astype(f32)
        total = total + full_in[a, 0, r].astype(f32) + full_in[a, 1, r].astype(f32)
        if r == 0:
            z_own[a] = total
        else:
            z_out[a, r - 1] = total.astype(bf16)
            go(third(a, r))

    def finish(a, out_ref):
        total = z_own[a]
        for r in range(1, quarters):
            slot = z_in.at[a, r - 1]
            remote(slot, slot, s_r3, (a, r - 1), z_dev(r)).wait_recv()
            total = total + z_in[a, r - 1].astype(f32)
        out_ref[...] = total.astype(bf16)

    for near, r in zip(GATHER_ORDER, SCATTER_ORDER):
        q = quarter(r)
        if near > 0:
            pass_on(1, near)
        parts[0, q] = jnp.dot(
            hw[...], weights[2, :, columns(q)], preferred_element_type=f32
        ).astype(bf16)
        send_first(0, r)

    for i, (near, r) in enumerate(zip(GATHER_ORDER, SCATTER_ORDER)):
        q = quarter(near)
        complete(1, near)
        term = contract_last(acts[1, q], weights[2, :, columns(q)])
        into[...] = term if i == 0 else into[...] + term
        add_first(0, r)

    @pl.loop(0, 4)
    def _(b):
        at = block_rows(b)
        gate_act, up_act, back = gate[at, :], up[at, :], into[at, :]
        active, slope = silu_parts(gate_act)
        term = jnp.sum(back * (active * up_act), axis=1, keepdims=True)
        route[at, :] = jnp.where(lane == expert, term, 0.0)
        scaled = scale_of(b) * back
        gate_grad, up_grad = scaled * up_act * slope, scaled * active
        gg[at, :] = gate_grad.astype(bf16)
        ug[at, :] = up_grad.astype(bf16)
        turned[0, :, at] = gate_grad.T.astype(bf16)
        turned[1, :, at] = up_grad.T.astype(bf16)

    for r in SCATTER_ORDER:
        q = quarter(r)
        total = jnp.dot(gg[...], weights[0, :, columns(q)], preferred_element_type=f32)
        total = total + jnp.dot(ug[...], weights[1, :, columns(q)], preferred_element_type=f32)
        parts[1, q] = total.astype(bf16)
        send_first(1, r)
    route_copies = [
        remote(route.at[place], route_in.at[i], s_rt, (i,), dev)
        for i, (place, dev) in enumerate(((at_x, x_dev), (at_y, y_dev), (at_d, diag_dev)))
    ]
    for copy in route_copies:
        go(copy)

    lent_grads = []
    for m in range(3):
        @pl.loop(0, quarters)
        def _(q, m=m):
            wg_out[m, :, columns(q)] = jnp.dot(
                turned[m, pl.ds(unit, unit), :], acts[m // 2, q], preferred_element_type=f32
            ).astype(bf16)

        lent_grads.append(remote(wg_out.at[m], wg_in.at[m], s_wg, (m,), twin))
        go(lent_grads[m])

    for r in SCATTER_ORDER:
        add_second(0, r)
    for r in SCATTER_ORDER[:2]:
        add_first(1, r)

    for copy in route_copies:
        copy.wait_recv()
    route_sum[...] = route[own, :] + route_in[0] + route_in[1] + route_in[2]
    slab = rows // quarters

    def slab_of(q):
        return pl.ds(pl.multiple_of(q * slab, slab), slab)

    slab_copies = []
    for s in range(1, quarters):
        slab_copies.append(remote(route_sum.at[slab_of(quarter(s))], route_z.at[quarters - 1 - s], s_rz, (quarters - 1 - s,), z_dev(s)))
        slab_copies[-1].start()

    for m, out_ref in enumerate((gg_ref, gu_ref, gd_ref)):
        lent_grads[m].wait_recv()

        @pl.loop(0, quarters)
        def _(q, m=m, out_ref=out_ref):
            total = jnp.dot(turned[m, pl.ds(0, unit), :], acts[m // 2, q], preferred_element_type=f32)
            out_ref[0, :, columns(q)] = (total + wg_in[m, :, columns(q)].astype(f32)).astype(bf16)

        if m < 2:
            add_first(1, SCATTER_ORDER[m + 2])
        add_second(1, SCATTER_ORDER[m])

    add_second(1, SCATTER_ORDER[3])
    finish(0, mixed_ref)
    total = route_sum[slab_of(z), :]
    for r in range(1, quarters):
        slot = route_z.at[r - 1]
        remote(slot, slot, s_rz, (r - 1,), z_dev(r)).wait_recv()
        total = total + route_z[r - 1]
    for copy in slab_copies:
        copy.wait_send()
    names = names_wide[slab_of(z), :]
    lane_slab = lax.broadcasted_iota(jnp.int32, (slab, 128), 1)
    picked = jnp.zeros((slab, 128), f32)
    for k in range(topk):
        match = lane_slab.astype(f32) == names[:, k : k + 1]
        value = jnp.sum(jnp.where(match, total, 0.0), axis=1, keepdims=True)
        picked = jnp.where(lane_slab == k, value, picked)
    route_sum[pl.ds(0, slab), :] = picked
    route_ref[...] = route_sum[...].T[:topk, :slab]
    finish(1, token_ref)
    for copy in started:
        copy.wait_send()


def deliver(*refs):
    count = len(refs) // 2
    for src, dst in zip(refs[:count], refs[count:]):
        dst[...] = src[...]


def dense_device(tokens, route_weight, expert_ids, gate_weight, up_weight, down_weight, grad_output):
    quarters = lax.axis_size("expert")
    rows, feat = tokens.shape
    unit, width = gate_weight.shape[1:]
    topk = expert_ids.shape[1]
    f32, bf16 = jnp.float32, jnp.bfloat16
    vmem = pl.BlockSpec(memory_space=pltpu.VMEM)
    hbm = pl.BlockSpec(memory_space=pl.ANY)
    every, both, half = 4 * rows, 2 * unit, rows // 2
    dma = pltpu.SemaphoreType.DMA
    grads = jax.ShapeDtypeStruct((1, unit, width), bf16)
    results = pl.pallas_call(
        dense_kernel,
        out_shape=(
            jax.ShapeDtypeStruct((rows, feat), bf16),
            jax.ShapeDtypeStruct((rows, feat), bf16),
            jax.ShapeDtypeStruct((topk, rows // quarters), f32),
            grads,
            grads,
            grads,
        ),
        in_specs=[hbm, vmem, vmem, hbm, hbm, hbm, hbm],
        out_specs=(vmem,) * 6,
        scratch_shapes=[
            pltpu.VMEM((2, quarters, every, feat), bf16),
            pltpu.VMEM((2, quarters, every, feat), bf16),
            pltpu.VMEM((3, both, width), bf16),
            pltpu.VMEM((every, 128), f32),
            pltpu.VMEM((rows, 128), f32),
            pltpu.VMEM((every, both), f32),
            pltpu.VMEM((every, both), f32),
            pltpu.VMEM((every, both), f32),
            pltpu.VMEM((every, both), bf16),
            pltpu.VMEM((every, both), bf16),
            pltpu.VMEM((every, both), bf16),
            pltpu.VMEM((3, both, every), bf16),
            pltpu.VMEM((2, 2, quarters, half, feat), bf16),
            pltpu.VMEM((2, 2, quarters, rows, feat), bf16),
            pltpu.VMEM((2, quarters - 1, rows, feat), bf16),
            pltpu.VMEM((2, quarters - 1, rows, feat), bf16),
            pltpu.VMEM((2, rows, feat), f32),
            pltpu.VMEM((every, 128), f32),
            pltpu.VMEM((3, rows, 128), f32),
            pltpu.VMEM((rows, 128), f32),
            pltpu.VMEM((quarters - 1, rows // quarters, 128), f32),
            pltpu.VMEM((3, unit, width), bf16),
            pltpu.VMEM((3, unit, width), bf16),
            dma((2, 2, quarters - 1)),
            dma((2, 2, 2, quarters)),
            dma((2, 2, 2, quarters)),
            dma((2, 3)),
            dma((2, 3)),
            dma((5,)),
            dma((2, 2, 2, quarters)),
            dma((2, 2, 2, quarters)),
            dma((2, 2, quarters - 1)),
            dma((2, 3)),
            dma((2, quarters - 1)),
            dma((2, 3)),
        ],
        compiler_params=pltpu.CompilerParams(
            collective_id=0, has_side_effects=True, vmem_limit_bytes=60 * 2**20
        ),
        cost_estimate=pl.CostEstimate(
            flops=18 * every * both * width, bytes_accessed=12 * unit * width, transcendentals=2 * every * both
        ),
    )(tokens, route_weight.T, expert_ids.T, gate_weight, up_weight, down_weight, grad_output)
    count = len(results)
    mixed, token_part, route_part, *weight_grads = pl.pallas_call(
        deliver,
        out_shape=tuple(jax.ShapeDtypeStruct(v.shape, v.dtype) for v in results),
        in_specs=[vmem] * count,
        out_specs=(vmem,) * count,
        compiler_params=pltpu.CompilerParams(vmem_limit_bytes=60 * 2**20),
    )(*results)
    return (mixed, token_part, route_part.T, *weight_grads)


def on_device(tokens, route_weight, expert_ids, *rest):
    shape = (lax.axis_size("dp"), lax.axis_size("expert"))
    experts = shape[0] // PIECES * shape[1]
    dense = shape == (8, 4) and experts == expert_ids.shape[1]
    body = dense_device if dense else slot_device
    return body(tokens, route_weight, expert_ids, *rest)


def solution(mesh):
    return jax.shard_map(
        on_device,
        mesh=mesh,
        in_specs=(
            P("dp", "expert"),
            P("dp", None),
            P("dp", None),
            P("expert", "dp", None),
            P("expert", "dp", None),
            P("expert", "dp", None),
            P("dp", "expert"),
        ),
        out_specs=(
            P("dp", "expert"),
            P("dp", "expert"),
            P(("dp", "expert"), None),
            P("expert", "dp", None),
            P("expert", "dp", None),
            P("expert", "dp", None),
        ),
        check_vma=False,
    )
```
